1024 devices in a mesh: comp: 32 (over z_hi, x, core), space: 32 (over z_lo, y).
Axes of the slice: x: 4, y: 8, z: 16 (z_hi: 4, z_lo: 4; z = z_hi * 4 + z_lo), core: 2. Of those that a mesh axis runs over, the one named last changes fastest.
Arguments:
- spectrum: float32 [288, 1024, 1024], P('comp', 'space'), may hold values from 0.01 to 1
- sea_mask: int32 [1024, 1024], P('space'), may hold values 0 or 1
- ice_flag: int32 [1024, 1024], P('space'), may hold values 0 or 1
- thickness: float32 [1024, 1024], P('space'), may hold values from 0.1 to 3
Outputs:
- updated: float32 [288, 1024, 1024], P('comp', 'space')
The draws below stay inside these ranges and needn't reach their ends.
All inputs are finite; a program needn't handle non-finite values. No bound on the sum of `sea_mask` or of `ice_flag` on one device may be relied on, other than what follows from the above.
Results may differ from the reference program's by a relative error of at most 0.00002.
Values sent between devices are 32-bit elements; how exact they have to be, the bound alone decides.
No kernel may reach another device: no remote copies, remote signals or barrier semaphores. Data moves between devices by JAX's collectives and lax.ppermute only.
A program may use at most 32 MiB of HBM per device.

```python
import math
import jax
import jax.numpy as jnp

ND = 36
NF = 8
NX = 1024
PSTEPS = 4
K = 288
NY = 1024


def with_ends(result, stream_key, smallest, top_value):
    longest = result.shape.index(max(result.shape))
    spots = []
    for shift in (0, 1):
        where = [jax.random.randint(jax.random.fold_in(stream_key, axis), (), 0, length) for axis, length in enumerate(result.shape)]
        where[longest] = (where[longest] + shift) % result.shape[longest]
        spots.append(tuple(where))
    return result.at[spots[0]].set(smallest).at[spots[1]].set(top_value)


def block_scale(stream_key, extent, pieces, low, high):
    loudness = 1.0
    for dim, blocks in pieces:
        steps = jax.random.uniform(jax.random.fold_in(jax.random.fold_in(stream_key, 6), dim), (blocks,), jnp.float32, low / len(pieces), high / len(pieces))
        loudness = loudness * jnp.repeat(jnp.exp(steps), extent[dim] // blocks).reshape((-1,) + (1,) * (len(extent) - 1 - dim))
    return loudness


def setup_inputs(seed: int = 0) -> dict:
    splits = jax.random.split(jax.random.key(seed), 5)
    return {
        "spectrum": jnp.clip(jnp.exp(math.log(1.0) - 4.6051702 * jax.random.uniform(splits[0], (K, NY, NX), jnp.float32) ** block_scale(splits[0], (K, NY, NX), ((0, 32), (1, 32)), -0.2, 0.2)), 0.01, 1.0),
        "sea_mask": with_ends((jax.random.randint(splits[1], (NY, NX), 0, 8) < 7).astype(jnp.int32), jax.random.fold_in(splits[1], 1), 0, 1),
        "ice_flag": with_ends((jax.random.randint(splits[2], (NY, NX), 0, 2) < 1).astype(jnp.int32), jax.random.fold_in(splits[2], 1), 0, 1),
        "thickness": jnp.clip(jnp.exp(math.log(3.0) - 3.4011974 * jax.random.uniform(splits[3], (NY, NX), jnp.float32) ** block_scale(splits[3], (NY, NX), ((0, 32),), -0.2, 0.2)), 0.1, 3.0),
    }


courant_top = 0.65
mixing_rate = 0.5
whitecap_rate = 2.0
ice_rate = 0.3


def comp_tables(first, count):
    index = first + jnp.arange(count, dtype=jnp.int32)
    freq_index = index // ND
    dir_index = index % ND
    ratio = jnp.power(jnp.float32(1.1), freq_index.astype(jnp.float32))
    courant = courant_top / ratio
    theta = (dir_index.astype(jnp.float32) + 0.5) * (2.0 * math.pi / ND)
    return courant * jnp.cos(theta), courant * jnp.sin(theta), ratio * ratio


def upwind(framed, speed_x, speed_y):
    middle = framed[:, 1:-1, 1:-1]
    west = framed[:, 1:-1, :-2]
    east = framed[:, 1:-1, 2:]
    south = framed[:, :-2, 1:-1]
    north = framed[:, 2:, 1:-1]
    to_east = jnp.maximum(speed_x, 0.0)[:, None, None]
    to_west = jnp.maximum(-speed_x, 0.0)[:, None, None]
    to_north = jnp.maximum(speed_y, 0.0)[:, None, None]
    to_south = jnp.maximum(-speed_y, 0.0)[:, None, None]
    return middle - to_east * (middle - west) - to_west * (middle - east) - to_north * (middle - south) - to_south * (middle - north)


def shift_freq(values, offset):
    zeros = jnp.zeros((abs(offset),) + values.shape[1:], values.dtype)
    if offset > 0:
        return jnp.concatenate([values[offset:], zeros], axis=0)
    return jnp.concatenate([zeros, values[:offset]], axis=0)


def source_mix(points):
    shaped = points.reshape((NF, ND) + points.shape[1:])
    neighbours = shift_freq(jnp.roll(shaped, -3, axis=1), 2) + shift_freq(jnp.roll(shaped, 3, axis=1), 2)
    neighbours = neighbours + shift_freq(jnp.roll(shaped, -1, axis=1), -2) + shift_freq(jnp.roll(shaped, 1, axis=1), -2)
    mixed = shaped + mixing_rate * shaped * (0.25 * neighbours - shaped)
    energy = jnp.mean(mixed, axis=(0, 1))
    ratio = jnp.power(jnp.float32(1.1), jnp.arange(NF, dtype=jnp.int32).astype(jnp.float32))
    weight = (ratio * ratio).reshape((NF, 1) + (1,) * (points.ndim - 1))
    return (mixed / (1.0 + whitecap_rate * energy[None, None] * weight)).reshape(points.shape)


def reference(spectrum, sea_mask, ice_flag, thickness):
    speed_x, speed_y, freq_sq = comp_tables(0, ND * NF)
    land = sea_mask.astype(jnp.float32)
    field = spectrum * land[None]
    for repeat in range(PSTEPS):
        framed = jnp.pad(field, ((0, 0), (1, 1), (1, 1)))
        field = upwind(framed, speed_x, speed_y) * land[None]
    mixed = source_mix(field)
    ice_depth = ice_flag.astype(jnp.float32) * thickness
    return mixed * jnp.exp(-ice_rate * ice_depth[None] * freq_sq[:, None, None])
```

```python
import functools
import math

import jax
import jax.numpy as jnp
import numpy as np
from jax import lax
from jax.experimental import pallas as pl
from jax.experimental.pallas import tpu as pltpu
from jax.sharding import PartitionSpec as P

ND = 36
NF = 8
PSTEPS = 4
QUARTERS = 4
NQ = ND // QUARTERS
GROUP = 8
EDGE = 3

courant_top = 0.65
mixing_rate = 0.5
whitecap_rate = 2.0
ice_rate = 0.3

VMEM_BYTES = 40 * 1024 * 1024


def tables():
    rows = np.zeros((NF * QUARTERS, 2 * NQ + 2), np.float32)
    for p in range(NF * QUARTERS):
        ratio = 1.1 ** (p // QUARTERS)
        for i in range(NQ):
            theta = 2.0 * math.pi * ((p % QUARTERS) * NQ + i + 0.5) / ND
            rows[p, i] = abs(courant_top / ratio * math.cos(theta))
            rows[p, NQ + i] = abs(courant_top / ratio * math.sin(theta))
        rows[p, 2 * NQ] = ratio * ratio
    return rows


def quarter():
    return lax.rem(lax.axis_index("comp"), QUARTERS)


def edge_rows(first_ref, last_ref, first_mask, last_mask, out_ref):
    def write(field_ref, mask_ref, low):
        land = mask_ref[low : low + PSTEPS].astype(jnp.float32)
        for i in range(NQ):
            out_ref[PSTEPS * i : PSTEPS * (i + 1)] = field_ref[i, low : low + PSTEPS] * land
        out_ref[PSTEPS * NQ :] = land

    @pl.when(quarter() < 2)
    def _():
        write(last_ref, last_mask, 8 - PSTEPS)

    @pl.when(quarter() >= 2)
    def _():
        write(first_ref, first_mask, 0)


def propagate(table_ref, field_ref, mask_ref, halo_ref, a_ref, b_ref, lo_ref, hi_ref, land, ext):
    p = lax.axis_index("comp")
    q = lax.rem(p, QUARTERS)
    rows, cols = mask_ref.shape
    half = rows // 2
    high = rows + 8

    def run(eastward, northward):
        own = 8 if northward else 0
        halo = 8 - PSTEPS if northward else rows
        rest = 0 if northward else rows + PSTEPS
        zeros = jnp.zeros((8 - PSTEPS, cols), jnp.float32)
        land[own : own + rows] = mask_ref[...].astype(jnp.float32)
        land[halo : halo + PSTEPS] = halo_ref[PSTEPS * NQ :]
        land[rest : rest + 8 - PSTEPS] = zeros
        ext[rest : rest + 8 - PSTEPS] = zeros
        column = lax.broadcasted_iota(jnp.int32, (1, cols), 1)
        inner = (column != (0 if eastward else cols - 1)).astype(jnp.float32)

        def component(i, carry):
            ext[own : own + rows] = field_ref[i] * land[own : own + rows]
            for r in range(PSTEPS):
                ext[halo + r : halo + r + 1] = halo_ref[pl.ds(PSTEPS * i + r, 1)]
            ax = table_ref[p, i]
            ay = table_ref[p, NQ + i]
            stay = 1.0 - ax - ay
            side = inner * ax
            f = ext[...]
            for _ in range(PSTEPS):
                along = pltpu.roll(f, 1 if eastward else cols - 1, 1)
                across = pltpu.roll(f, 1 if northward else high - 1, 0)
                f = (stay * f + side * along + ay * across) * land[...]
            a_ref[i] = f[own : own + half]
            b_ref[i] = f[own + half : own + rows]

            @pl.when(i < EDGE)
            def _():
                lo_ref[i] = f[own : own + rows]

            @pl.when(i >= NQ - EDGE)
            def _():
                hi_ref[i - (NQ - EDGE)] = f[own : own + rows]

            return carry

        lax.fori_loop(0, NQ, component, 0)

    for k, (eastward, northward) in enumerate(
        ((True, True), (False, True), (False, False), (True, False))
    ):
        pl.when(q == k)(functools.partial(run, eastward, northward))


def at(low_ref, mid_ref, top_ref, i, rows, low_rows):
    if i < 0:
        return low_ref[i + EDGE, low_rows]
    if i >= NQ:
        return top_ref[i - NQ, low_rows]
    return mid_ref[i, rows]


def sums(a_ref, b_ref, low_ref, top_ref, s1_ref, s3_ref):
    half = a_ref.shape[1]
    for t in range(0, half, 8):
        rows = pl.ds(t, 8)
        a = lambda i: at(low_ref, a_ref, top_ref, i, rows, rows)
        b = lambda i: at(low_ref, b_ref, top_ref, i, rows, pl.ds(half + t, 8))
        for i in range(NQ):
            s1_ref[i, rows] = a(i - 1) + a(i + 1)
            s3_ref[i, rows] = b(i - 3) + b(i + 3)


def partial_energy(a_ref, b_ref, low_ref, top_ref, u_ref, d_ref, out_ref, prev_ref, next_ref):
    half, cols = a_ref.shape[1:]
    width = cols // GROUP
    for t in range(0, 2 * half, 8):
        mid, other, s = (a_ref, u_ref, t) if t < half else (b_ref, d_ref, t - half)
        e = lambda i: at(low_ref, mid, top_ref, i, pl.ds(s, 8), pl.ds(t, 8))
        total = jnp.zeros((8, cols), jnp.float32)
        for i in range(NQ):
            around = (e(i - 3) + e(i + 3)) + (e(i - 1) + e(i + 1))
            crossed = 0.25 * mixing_rate * other[i, pl.ds(s, 8)] * around
            total = total + (e(i) - mixing_rate * e(i) * e(i) + crossed)
        for g in range(GROUP):
            out_ref[g, t : t + 8] = total[:, g * width : (g + 1) * width]
    prev_ref[:EDGE] = u_ref[:EDGE]
    prev_ref[EDGE] = d_ref[0]
    next_ref[:EDGE] = u_ref[NQ - EDGE :]
    next_ref[EDGE] = d_ref[NQ - 1]


def finish(table_ref, a_ref, b_ref, u_ref, d_ref, low_ref, top_ref, s1_ref, s3_ref, energy_ref, ice_ref, thick_ref, out_ref):
    p = lax.axis_index("comp")
    fsq = table_ref[p, 2 * NQ]
    half = a_ref.shape[1]
    for t in range(0, 2 * half, 8):
        rows = pl.ds(t, 8)
        energy = jnp.concatenate([energy_ref[g, rows] for g in range(GROUP)], axis=1) * (1.0 / (ND * NF))
        depth = ice_ref[rows].astype(jnp.float32) * thick_ref[rows]
        factor = jnp.exp(-ice_rate * depth * fsq) / (1.0 + whitecap_rate * energy * fsq)
        for i in range(NQ):
            if t < half:
                e = a_ref[i, rows]
                u = lambda k: at(low_ref, u_ref, top_ref, k, rows, rows)
                near = s1_ref[i, rows] + (u(i - 3) + u(i + 3))
            else:
                s = pl.ds(t - half, 8)
                e = b_ref[i, s]
                d = lambda k: (
                    low_ref[EDGE, s] if k < 0 else top_ref[EDGE, s] if k >= NQ else d_ref[k, s]
                )
                near = s3_ref[i, s] + (d(i - 1) + d(i + 1))
            out_ref[i, rows] = (e + mixing_rate * e * (0.25 * near - e)) * factor


def in_vmem(count):
    return [pl.BlockSpec(memory_space=pltpu.VMEM)] * count


def in_smem():
    return [pl.BlockSpec(memory_space=pltpu.SMEM)]


def call(kernel, outs, table, count, scratch=()):
    shapes = [jax.ShapeDtypeStruct(s, jnp.float32) for s in outs]
    specs = in_vmem(len(outs))
    return pl.pallas_call(
        kernel,
        out_shape=shapes,
        in_specs=(in_smem() if table else []) + in_vmem(count),
        out_specs=specs,
        scratch_shapes=list(scratch),
        compiler_params=pltpu.CompilerParams(vmem_limit_bytes=VMEM_BYTES),
        name=kernel.__name__,
    )


def body(spectrum, sea_mask, ice_flag, thickness):
    comps, rows, cols = spectrum.shape
    half = rows // 2
    n_comp = lax.axis_size("comp")
    n_space = lax.axis_size("space")
    table = jnp.asarray(tables())

    def move(value, step):
        pairs = [(p, p + step) for p in range(n_comp) if 0 <= p + step < n_comp]
        return lax.ppermute(value, "comp", pairs)

    def turn(value, step):
        pairs = [(p, p // QUARTERS * QUARTERS + (p + step) % QUARTERS) for p in range(n_comp)]
        return lax.ppermute(value, "comp", pairs)

    message = pl.pallas_call(
        edge_rows,
        grid=(1,),
        out_shape=jax.ShapeDtypeStruct((PSTEPS * (comps + 1), cols), jnp.float32),
        in_specs=[
            pl.BlockSpec((comps, 8, cols), lambda g: (0, 0, 0)),
            pl.BlockSpec((comps, 8, cols), lambda g: (0, rows // 8 - 1, 0)),
            pl.BlockSpec((8, cols), lambda g: (0, 0)),
            pl.BlockSpec((8, cols), lambda g: (rows // 8 - 1, 0)),
        ],
        out_specs=pl.BlockSpec((PSTEPS * (comps + 1), cols), lambda g: (0, 0)),
        name="edge_rows",
    )(spectrum, spectrum, sea_mask, sea_mask)
    pairs = []
    for p in range(n_comp):
        step = 1 if p % QUARTERS < 2 else -1
        pairs += [
            (p * n_space + s, p * n_space + s + step) for s in range(n_space) if 0 <= s + step < n_space
        ]
    halo = lax.ppermute(message, ("comp", "space"), pairs)

    part = (comps, half, cols)
    edge = (EDGE, rows, cols)
    a, b, lo, hi = call(
        propagate,
        [part, part, edge, edge],
        True,
        3,
        [pltpu.VMEM((rows + 8, cols), jnp.float32), pltpu.VMEM((rows + 8, cols), jnp.float32)],
    )(table, spectrum, sea_mask, halo)

    u = move(a, -GROUP)
    d = move(b, GROUP)
    top = turn(lo, -1)
    low = turn(hi, 1)
    s1, s3 = call(sums, [part, part], False, 4)(a, b, low, top)
    s1 = move(s1, GROUP)
    s3 = move(s3, -GROUP)

    edges = (EDGE + 1, half, cols)
    share, to_prev, to_next = call(
        partial_energy, [(GROUP, rows, cols // GROUP), edges, edges], False, 6
    )(a, b, low, top, u, d)
    top_u = turn(to_prev, -1)
    low_u = turn(to_next, 1)

    near = [list(range(g, g + GROUP)) for g in range(0, n_comp, GROUP)]
    far = [list(range(g, n_comp, GROUP)) for g in range(GROUP)]

    def swap(value, groups):
        return lax.all_to_all(value, "comp", 0, 0, axis_index_groups=groups, tiled=True)

    share = jnp.sum(swap(share, near), axis=0)
    share = swap(jnp.broadcast_to(share[None], (n_comp // GROUP,) + share.shape), far)
    share = jnp.sum(share, axis=0)
    energy = swap(jnp.broadcast_to(share[None], (GROUP,) + share.shape), near)

    (out,) = call(finish, [(comps, rows, cols)], True, 11)(
        table, a, b, u, d, low_u, top_u, s1, s3, energy, ice_flag, thickness
    )
    return out


def solution(mesh):
    in_specs = (P("comp", "space", None), P("space", None), P("space", None), P("space", None))
    out_specs = P("comp", "space", None)
    return jax.shard_map(body, mesh=mesh, in_specs=in_specs, out_specs=out_specs, check_vma=False)
```

```python
import functools
import math

import jax
import jax.numpy as jnp
import numpy as np
from jax import lax
from jax.experimental import pallas as pl
from jax.experimental.pallas import tpu as pltpu
from jax.sharding import PartitionSpec as P

ND = 36
NF = 8
PSTEPS = 4
QUARTERS = 4
NQ = ND // QUARTERS
GROUP = 8
EDGE = 3

courant_top = 0.65
mixing_rate = 0.5
whitecap_rate = 2.0
ice_rate = 0.3

VMEM_BYTES = 16 * 1024 * 1024


def tables():
    rows = np.zeros((NF * QUARTERS, 2 * NQ + 2), np.float32)
    for p in range(NF * QUARTERS):
        ratio = 1.1 ** (p // QUARTERS)
        for i in range(NQ):
            theta = 2.0 * math.pi * ((p % QUARTERS) * NQ + i + 0.5) / ND
            rows[p, i] = abs(courant_top / ratio * math.cos(theta))
            rows[p, NQ + i] = abs(courant_top / ratio * math.sin(theta))
        rows[p, 2 * NQ] = ratio * ratio
    return rows


def quarter():
    return lax.rem(lax.axis_index("comp"), QUARTERS)


def edge_rows(first_ref, last_ref, first_mask, last_mask, out_ref):
    def write(field_ref, mask_ref, low):
        land = mask_ref[low : low + PSTEPS].astype(jnp.float32)
        for i in range(NQ):
            out_ref[PSTEPS * i : PSTEPS * (i + 1)] = field_ref[i, low : low + PSTEPS] * land
        out_ref[PSTEPS * NQ :] = land

    @pl.when(quarter() < 2)
    def _():
        write(last_ref, last_mask, 8 - PSTEPS)

    @pl.when(quarter() >= 2)
    def _():
        write(first_ref, first_mask, 0)


def propagate(table_ref, field_ref, mask_ref, halo_ref, a_ref, b_ref, lo_ref, hi_ref, land, ext):
    p = lax.axis_index("comp")
    q = lax.rem(p, QUARTERS)
    rows, cols = mask_ref.shape
    half = rows // 2
    high = rows + 8

    def run(eastward, northward):
        own = 8 if northward else 0
        halo = 8 - PSTEPS if northward else rows
        rest = 0 if northward else rows + PSTEPS
        zeros = jnp.zeros((8 - PSTEPS, cols), jnp.float32)
        land[own : own + rows] = mask_ref[...].astype(jnp.float32)
        land[halo : halo + PSTEPS] = halo_ref[PSTEPS * NQ :]
        land[rest : rest + 8 - PSTEPS] = zeros
        ext[rest : rest + 8 - PSTEPS] = zeros
        column = lax.broadcasted_iota(jnp.int32, (1, cols), 1)
        inner = (column != (0 if eastward else cols - 1)).astype(jnp.float32)

        def component(i, carry):
            ext[own : own + rows] = field_ref[i] * land[own : own + rows]
            for r in range(PSTEPS):
                ext[halo + r : halo + r + 1] = halo_ref[pl.ds(PSTEPS * i + r, 1)]
            ax = table_ref[p, i]
            ay = table_ref[p, NQ + i]
            stay = 1.0 - ax - ay
            side = inner * ax
            f = ext[...]
            for _ in range(PSTEPS):
                along = pltpu.roll(f, 1 if eastward else cols - 1, 1)
                across = pltpu.roll(f, 1 if northward else high - 1, 0)
                f = (stay * f + side * along + ay * across) * land[...]
            a_ref[i] = f[own : own + half]
            b_ref[i] = f[own + half : own + rows]

            @pl.when(i < EDGE)
            def _():
                lo_ref[i] = f[own : own + rows]

            @pl.when(i >= NQ - EDGE)
            def _():
                hi_ref[i - (NQ - EDGE)] = f[own : own + rows]

            return carry

        lax.fori_loop(0, NQ, component, 0)

    for k, (eastward, northward) in enumerate(
        ((True, True), (False, True), (False, False), (True, False))
    ):
        pl.when(q == k)(functools.partial(run, eastward, northward))


def at(low_ref, mid_ref, top_ref, i, rows, low_rows):
    if i < 0:
        return low_ref[i + EDGE, low_rows]
    if i >= NQ:
        return top_ref[i - NQ, low_rows]
    return mid_ref[i, rows]


def attenuation(table_ref, ice_ref, thick_ref, out_ref):
    fsq = table_ref[lax.axis_index("comp"), 2 * NQ]
    depth = ice_ref[...].astype(jnp.float32) * thick_ref[...]
    out_ref[...] = jnp.exp(-ice_rate * depth * fsq)


def half_way(a_ref, b_ref, low_ref, top_ref, u_ref, d_ref, s1_ref, s3_ref, out_ref, prev_ref, next_ref):
    half, cols = a_ref.shape[1:]
    width = cols // GROUP
    for t in range(0, 2 * half, 8):
        first = t < half
        mid, other, s = (a_ref, u_ref, t) if first else (b_ref, d_ref, t - half)
        e = lambda i: at(low_ref, mid, top_ref, i, pl.ds(s, 8), pl.ds(t, 8))
        total = jnp.zeros((8, cols), jnp.float32)
        for i in range(NQ):
            near, far = e(i - 1) + e(i + 1), e(i - 3) + e(i + 3)
            if first:
                s1_ref[i, pl.ds(s, 8)] = near
            else:
                s3_ref[i, pl.ds(s, 8)] = far
            crossed = 0.25 * mixing_rate * other[i, pl.ds(s, 8)] * (near + far)
            total = total + (e(i) - mixing_rate * e(i) * e(i) + crossed)
        for g in range(GROUP):
            out_ref[g, t : t + 8] = total[:, g * width : (g + 1) * width]
    prev_ref[:EDGE] = u_ref[:EDGE]
    prev_ref[EDGE] = d_ref[0]
    next_ref[:EDGE] = u_ref[NQ - EDGE :]
    next_ref[EDGE] = d_ref[NQ - 1]


def total_to_all(parts_ref, out_ref):
    total = parts_ref[0]
    for k in range(1, parts_ref.shape[0]):
        total = total + parts_ref[k]
    for k in range(out_ref.shape[0]):
        out_ref[k] = total


def finish(table_ref, a_ref, b_ref, u_ref, d_ref, low_ref, top_ref, s1_ref, s3_ref, energy_ref, att_ref, out_ref):
    p = lax.axis_index("comp")
    fsq = table_ref[p, 2 * NQ]
    half = a_ref.shape[1]
    for t in range(0, 2 * half, 8):
        rows = pl.ds(t, 8)
        energy = jnp.concatenate([energy_ref[g, rows] for g in range(GROUP)], axis=1) * (1.0 / (ND * NF))
        factor = att_ref[rows] / (1.0 + whitecap_rate * energy * fsq)
        for i in range(NQ):
            if t < half:
                e = a_ref[i, rows]
                u = lambda k: at(low_ref, u_ref, top_ref, k, rows, rows)
                near = s1_ref[i, rows] + (u(i - 3) + u(i + 3))
            else:
                s = pl.ds(t - half, 8)
                e = b_ref[i, s]
                d = lambda k: (
                    low_ref[EDGE, s] if k < 0 else top_ref[EDGE, s] if k >= NQ else d_ref[k, s]
                )
                near = s3_ref[i, s] + (d(i - 1) + d(i + 1))
            out_ref[i, rows] = (e + mixing_rate * e * (0.25 * near - e)) * factor


def in_vmem(count):
    return [pl.BlockSpec(memory_space=pltpu.VMEM)] * count


def in_smem():
    return [pl.BlockSpec(memory_space=pltpu.SMEM)]


def call(kernel, outs, table, count, scratch=()):
    shapes = [jax.ShapeDtypeStruct(s, jnp.float32) for s in outs]
    specs = in_vmem(len(outs))
    return pl.pallas_call(
        kernel,
        out_shape=shapes,
        in_specs=(in_smem() if table else []) + in_vmem(count),
        out_specs=specs,
        scratch_shapes=list(scratch),
        compiler_params=pltpu.CompilerParams(vmem_limit_bytes=VMEM_BYTES),
        name=kernel.__name__,
    )


def body(spectrum, sea_mask, ice_flag, thickness):
    comps, rows, cols = spectrum.shape
    half = rows // 2
    n_comp = lax.axis_size("comp")
    n_space = lax.axis_size("space")
    table = jnp.asarray(tables())

    def move(value, step):
        pairs = [(p, p + step) for p in range(n_comp) if 0 <= p + step < n_comp]
        return lax.ppermute(value, "comp", pairs)

    def turn(value, step):
        pairs = [(p, p // QUARTERS * QUARTERS + (p + step) % QUARTERS) for p in range(n_comp)]
        return lax.ppermute(value, "comp", pairs)

    message = pl.pallas_call(
        edge_rows,
        grid=(1,),
        out_shape=jax.ShapeDtypeStruct((PSTEPS * (comps + 1), cols), jnp.float32),
        in_specs=[
            pl.BlockSpec((comps, 8, cols), lambda g: (0, 0, 0)),
            pl.BlockSpec((comps, 8, cols), lambda g: (0, rows // 8 - 1, 0)),
            pl.BlockSpec((8, cols), lambda g: (0, 0)),
            pl.BlockSpec((8, cols), lambda g: (rows // 8 - 1, 0)),
        ],
        out_specs=pl.BlockSpec((PSTEPS * (comps + 1), cols), lambda g: (0, 0)),
        name="edge_rows",
    )(spectrum, spectrum, sea_mask, sea_mask)
    pairs = []
    for p in range(n_comp):
        step = 1 if p % QUARTERS < 2 else -1
        pairs += [
            (p * n_space + s, p * n_space + s + step) for s in range(n_space) if 0 <= s + step < n_space
        ]
    halo = lax.ppermute(message, ("comp", "space"), pairs)

    part = (comps, half, cols)
    edge = (EDGE, rows, cols)
    a, b, lo, hi = call(
        propagate,
        [part, part, edge, edge],
        True,
        3,
        [pltpu.VMEM((rows + 8, cols), jnp.float32), pltpu.VMEM((rows + 8, cols), jnp.float32)],
    )(table, spectrum, sea_mask, halo)

    u = move(a, -GROUP)
    d = move(b, GROUP)
    top = turn(lo, -1)
    low = turn(hi, 1)
    edges = (EDGE + 1, half, cols)
    s1, s3, share, to_prev, to_next = call(
        half_way, [part, part, (GROUP, rows, cols // GROUP), edges, edges], False, 6
    )(a, b, low, top, u, d)
    s1 = move(s1, GROUP)
    s3 = move(s3, -GROUP)
    (att,) = call(attenuation, [(rows, cols)], True, 2)(table, ice_flag, thickness)
    top_u = turn(to_prev, -1)
    low_u = turn(to_next, 1)

    near = [list(range(g, g + GROUP)) for g in range(0, n_comp, GROUP)]
    far = [list(range(g, n_comp, GROUP)) for g in range(GROUP)]

    def swap(value, groups):
        return lax.all_to_all(value, "comp", 0, 0, axis_index_groups=groups, tiled=True)

    def spread(value, copies):
        return call(total_to_all, [(copies,) + value.shape[1:]], False, 1)(value)[0]

    share = spread(swap(share, near), n_comp // GROUP)
    energy = swap(spread(swap(share, far), GROUP), near)

    (out,) = call(finish, [(comps, rows, cols)], True, 10)(
        table, a, b, u, d, low_u, top_u, s1, s3, energy, att
    )
    return out


def solution(mesh):
    in_specs = (P("comp", "space", None), P("space", None), P("space", None), P("space", None))
    out_specs = P("comp", "space", None)
    return jax.shard_map(body, mesh=mesh, in_specs=in_specs, out_specs=out_specs, check_vma=False)
```

```python
import functools
import math

import jax
import jax.numpy as jnp
import numpy as np
from jax import lax
from jax.experimental import pallas as pl
from jax.experimental.pallas import tpu as pltpu
from jax.sharding import PartitionSpec as P

ND = 36
NF = 8
PSTEPS = 4
QUARTERS = 4
NQ = ND // QUARTERS
GROUP = 8
EDGE = 3
Z_LOW = 4

courant_top = 0.65
mixing_rate = 0.5
whitecap_rate = 2.0
ice_rate = 0.3

VMEM_BYTES = 12 * 1024 * 1024


def tables():
    rows = np.zeros((NF * QUARTERS, 2 * NQ + 2), np.float32)
    for p in range(NF * QUARTERS):
        ratio = 1.1 ** (p // QUARTERS)
        for i in range(NQ):
            theta = 2.0 * math.pi * ((p % QUARTERS) * NQ + i + 0.5) / ND
            rows[p, i] = abs(courant_top / ratio * math.cos(theta))
            rows[p, NQ + i] = abs(courant_top / ratio * math.sin(theta))
        rows[p, 2 * NQ] = ratio * ratio
    return rows


def quarter():
    return lax.rem(lax.axis_index("comp"), QUARTERS)


def climbs(space, count):
    return 2 * space < count


def by_direction(kernel):
    here = climbs(lax.axis_index("space"), lax.axis_size("space"))
    pl.when(here)(lambda: kernel(True))
    pl.when(jnp.logical_not(here))(lambda: kernel(False))


def by_place(kernel):
    place = lax.axis_index("space") * Z_LOW // lax.axis_size("space")
    for k in range(Z_LOW):
        pl.when(place == k)(functools.partial(kernel, k))


def edge_rows(first_ref, last_ref, first_mask, last_mask, out_ref):
    def write(field_ref, mask_ref, low):
        land = mask_ref[low : low + PSTEPS].astype(jnp.float32)
        for i in range(NQ):
            out_ref[PSTEPS * i : PSTEPS * (i + 1)] = field_ref[i, low : low + PSTEPS] * land
        out_ref[PSTEPS * NQ :] = land

    @pl.when(quarter() < 2)
    def _():
        write(last_ref, last_mask, 8 - PSTEPS)

    @pl.when(quarter() >= 2)
    def _():
        write(first_ref, first_mask, 0)


def propagate(table_ref, field_ref, mask_ref, halo_ref, out_ref, lo_ref, hi_ref, land, ext):
    p = lax.axis_index("comp")
    q = lax.rem(p, QUARTERS)
    rows, cols = mask_ref.shape
    high = rows + 8

    def run(eastward, northward):
        own = 8 if northward else 0
        halo = 8 - PSTEPS if northward else rows
        rest = 0 if northward else rows + PSTEPS
        zeros = jnp.zeros((8 - PSTEPS, cols), jnp.float32)
        land[own : own + rows] = mask_ref[...].astype(jnp.float32)
        land[halo : halo + PSTEPS] = halo_ref[PSTEPS * NQ :]
        land[rest : rest + 8 - PSTEPS] = zeros
        ext[rest : rest + 8 - PSTEPS] = zeros
        column = lax.broadcasted_iota(jnp.int32, (1, cols), 1)
        inner = (column != (0 if eastward else cols - 1)).astype(jnp.float32)

        def component(i, carry):
            ext[own : own + rows] = field_ref[i] * land[own : own + rows]
            for r in range(PSTEPS):
                ext[halo + r : halo + r + 1] = halo_ref[pl.ds(PSTEPS * i + r, 1)]
            ax = table_ref[p, i]
            ay = table_ref[p, NQ + i]
            stay = 1.0 - ax - ay
            side = inner * ax
            f = ext[...]
            for _ in range(PSTEPS):
                along = pltpu.roll(f, 1 if eastward else cols - 1, 1)
                across = pltpu.roll(f, 1 if northward else high - 1, 0)
                f = (stay * f + side * along + ay * across) * land[...]
            out_ref[i] = f[own : own + rows]

            @pl.when(i < EDGE)
            def _():
                lo_ref[i] = f[own : own + rows]

            @pl.when(i >= NQ - EDGE)
            def _():
                hi_ref[i - (NQ - EDGE)] = f[own : own + rows]

            return carry

        lax.fori_loop(0, NQ, component, 0)

    for k, (eastward, northward) in enumerate(
        ((True, True), (False, True), (False, False), (True, False))
    ):
        pl.when(q == k)(functools.partial(run, eastward, northward))


def at(low_ref, mid_ref, top_ref, i, rows):
    if i < 0:
        return low_ref[i + EDGE, rows]
    if i >= NQ:
        return top_ref[i - NQ, rows]
    return mid_ref[i, rows]


def sums(table_ref, e_ref, low_ref, top_ref, ice_ref, thick_ref, out_ref, att_ref):
    fsq = table_ref[lax.axis_index("comp"), 2 * NQ]
    depth = ice_ref[...].astype(jnp.float32) * thick_ref[...]
    att_ref[...] = jnp.exp(-ice_rate * depth * fsq)

    def write(climbed):
        step = 3 if climbed else 1
        for t in range(0, e_ref.shape[1], 8):
            rows = pl.ds(t, 8)
            e = lambda i: at(low_ref, e_ref, top_ref, i, rows)
            for i in range(NQ):
                out_ref[i, rows] = e(i - step) + e(i + step)

    by_direction(write)


def half_way(e_ref, low_ref, top_ref, r_ref, share_ref, prev_ref, next_ref):
    rows, cols = e_ref.shape[1:]
    width = cols // GROUP
    for t in range(0, rows, 8):
        there = pl.ds(t, 8)
        e = lambda i: at(low_ref, e_ref, top_ref, i, there)
        total = jnp.zeros((8, cols), jnp.float32)
        for i in range(NQ):
            around = (e(i - 1) + e(i + 1)) + (e(i - 3) + e(i + 3))
            crossed = 0.25 * mixing_rate * r_ref[i, there] * around
            total = total + (e(i) - mixing_rate * e(i) * e(i) + crossed)
        for g in range(GROUP):
            share_ref[g, there] = total[:, g * width : (g + 1) * width]
    prev_ref[...] = r_ref[:EDGE]
    next_ref[...] = r_ref[NQ - EDGE :]


def total_to_all(parts_ref, out_ref):
    total = parts_ref[0]
    for k in range(1, parts_ref.shape[0]):
        total = total + parts_ref[k]
    for k in range(out_ref.shape[0]):
        out_ref[k] = total


def finish(
    table_ref, e_ref, r_ref, low_ref, top_ref, inner_ref, outer_ref, energy_ref, att_ref, told_ref, out_ref
):
    fsq = table_ref[lax.axis_index("comp"), 2 * NQ]

    def write(climbed, s_ref):
        step = 1 if climbed else 3
        for t in range(0, e_ref.shape[1], 8):
            rows = pl.ds(t, 8)
            energy = jnp.concatenate([energy_ref[g, rows] for g in range(GROUP)], axis=1) * (1.0 / (ND * NF))
            factor = att_ref[rows] / (1.0 + whitecap_rate * energy * fsq)
            raw = lambda i: at(low_ref, r_ref, top_ref, i, rows)
            for i in range(NQ):
                e = e_ref[i, rows]
                around = s_ref[i, rows] + (raw(i - step) + raw(i + step))
                out_ref[i, rows] = (e + mixing_rate * e * (0.25 * around - e)) * factor

    by_place(lambda k: write(k < 2, outer_ref if k in (0, 3) else inner_ref))


def in_vmem(count):
    return [pl.BlockSpec(memory_space=pltpu.VMEM)] * count


def in_smem():
    return [pl.BlockSpec(memory_space=pltpu.SMEM)]


def call(kernel, outs, table, count, scratch=()):
    shapes = [jax.ShapeDtypeStruct(s, jnp.float32) for s in outs]
    specs = in_vmem(len(outs))
    return pl.pallas_call(
        kernel,
        out_shape=shapes,
        in_specs=(in_smem() if table else []) + in_vmem(count),
        out_specs=specs,
        scratch_shapes=list(scratch),
        compiler_params=pltpu.CompilerParams(vmem_limit_bytes=VMEM_BYTES),
        cost_estimate=pl.CostEstimate(flops=1024, bytes_accessed=1024, transcendentals=0),
        name=kernel.__name__,
    )


def body(spectrum, sea_mask, ice_flag, thickness):
    comps, rows, cols = spectrum.shape
    n_comp = lax.axis_size("comp")
    n_space = lax.axis_size("space")
    table = jnp.asarray(tables())

    def place(s):
        return s * Z_LOW // n_space

    def move(value, first, places):
        pairs = []
        for p in range(n_comp):
            for s in range(n_space):
                to = p + (GROUP if climbs(s, n_space) == first else -GROUP)
                if 0 <= to < n_comp and place(s) in places:
                    pairs.append((p * n_space + s, to * n_space + s))
        return lax.ppermute(value, ("comp", "space"), pairs)

    def tell(value):
        pairs = []
        for p in range(n_comp):
            for s in range(n_space):
                step = n_space // Z_LOW * (1 if place(s) == 2 else -1)
                if place(s) in (1, 2):
                    pairs.append((p * n_space + s, p * n_space + s + step))
        return lax.ppermute(value, ("comp", "space"), pairs)

    def after(value, *others):
        return lax.optimization_barrier((value, *others))[0]

    def turn(value, step):
        pairs = [(p, p // QUARTERS * QUARTERS + (p + step) % QUARTERS) for p in range(n_comp)]
        return lax.ppermute(value, "comp", pairs)

    message = pl.pallas_call(
        edge_rows,
        grid=(1,),
        out_shape=jax.ShapeDtypeStruct((PSTEPS * (comps + 1), cols), jnp.float32),
        in_specs=[
            pl.BlockSpec((comps, 8, cols), lambda g: (0, 0, 0)),
            pl.BlockSpec((comps, 8, cols), lambda g: (0, rows // 8 - 1, 0)),
            pl.BlockSpec((8, cols), lambda g: (0, 0)),
            pl.BlockSpec((8, cols), lambda g: (rows // 8 - 1, 0)),
        ],
        out_specs=pl.BlockSpec((PSTEPS * (comps + 1), cols), lambda g: (0, 0)),
        name="edge_rows",
    )(spectrum, spectrum, sea_mask, sea_mask)
    pairs = []
    for p in range(n_comp):
        step = 1 if p % QUARTERS < 2 else -1
        pairs += [
            (p * n_space + s, p * n_space + s + step) for s in range(n_space) if 0 <= s + step < n_space
        ]
    halo = lax.ppermute(message, ("comp", "space"), pairs)

    whole = (comps, rows, cols)
    edge = (EDGE, rows, cols)
    scratch = pltpu.VMEM((rows + 8, cols), jnp.float32)
    e, lo, hi = call(propagate, [whole, edge, edge], True, 3, [scratch, scratch])(
        table, spectrum, sea_mask, halo
    )
    received = move(e, True, (0, 1, 2, 3))
    top = turn(lo, -1)
    low = turn(hi, 1)
    out, att = call(sums, [whole, (rows, cols)], True, 5)(table, e, low, top, ice_flag, thickness)
    out, received = lax.optimization_barrier((out, received))
    inner = move(out, False, (1, 2))

    share, to_prev, to_next = call(half_way, [(GROUP, rows, cols // GROUP), edge, edge], False, 4)(
        e, low, top, received
    )
    near = [list(range(g, g + GROUP)) for g in range(0, n_comp, GROUP)]
    far = [list(range(g, n_comp, GROUP)) for g in range(GROUP)]

    def swap(value, groups):
        return lax.all_to_all(value, "comp", 0, 0, axis_index_groups=groups, tiled=True)

    def spread(value, copies):
        return call(total_to_all, [(copies,) + value.shape[1:]], False, 1)(value)[0]

    share = swap(share, near)
    top = turn(after(to_prev, share), -1)
    low = turn(after(to_next, share), 1)
    share = swap(spread(share, n_comp // GROUP), far)
    share, inner = lax.optimization_barrier((share, inner))
    told = tell(share[0])
    out, share, told = lax.optimization_barrier((out, share, told))
    outer = move(out, False, (0, 3))
    energy = swap(spread(share, GROUP), near)

    (updated,) = call(finish, [whole], True, 9)(
        table, e, received, low, top, inner, outer, energy, att, told
    )
    return updated


def solution(mesh):
    in_specs = (P("comp", "space", None), P("space", None), P("space", None), P("space", None))
    out_specs = P("comp", "space", None)
    return jax.shard_map(body, mesh=mesh, in_specs=in_specs, out_specs=out_specs, check_vma=False)
```

```python
import functools
import math

import jax
import jax.numpy as jnp
import numpy as np
from jax import lax
from jax.experimental import pallas as pl
from jax.experimental.pallas import tpu as pltpu
from jax.sharding import PartitionSpec as P

ND = 36
NF = 8
PSTEPS = 4
QUARTERS = 4
NQ = ND // QUARTERS
GROUP = 8
EDGE = 3
Z_LOW = 4

courant_top = 0.65
mixing_rate = 0.5
whitecap_rate = 2.0
ice_rate = 0.3

VMEM_BYTES = 12 * 1024 * 1024


def tables():
    rows = np.zeros((NF * QUARTERS, 2 * NQ + 2), np.float32)
    for p in range(NF * QUARTERS):
        ratio = 1.1 ** (p // QUARTERS)
        for i in range(NQ):
            theta = 2.0 * math.pi * ((p % QUARTERS) * NQ + i + 0.5) / ND
            rows[p, i] = abs(courant_top / ratio * math.cos(theta))
            rows[p, NQ + i] = abs(courant_top / ratio * math.sin(theta))
        rows[p, 2 * NQ] = ratio * ratio
    return rows


def quarter():
    return lax.rem(lax.axis_index("comp"), QUARTERS)


def climbs(space, count):
    return 2 * space < count


def by_direction(kernel):
    here = climbs(lax.axis_index("space"), lax.axis_size("space"))
    pl.when(here)(lambda: kernel(True))
    pl.when(jnp.logical_not(here))(lambda: kernel(False))


def by_place(kernel):
    place = lax.axis_index("space") * Z_LOW // lax.axis_size("space")
    for k in range(Z_LOW):
        pl.when(place == k)(functools.partial(kernel, k))


def edge_rows(first_ref, last_ref, first_mask, last_mask, out_ref):
    def write(field_ref, mask_ref, low):
        land = mask_ref[low : low + PSTEPS].astype(jnp.float32)
        for i in range(NQ):
            out_ref[PSTEPS * i : PSTEPS * (i + 1)] = field_ref[i, low : low + PSTEPS] * land
        out_ref[PSTEPS * NQ :] = land

    @pl.when(quarter() < 2)
    def _():
        write(last_ref, last_mask, 8 - PSTEPS)

    @pl.when(quarter() >= 2)
    def _():
        write(first_ref, first_mask, 0)


def by_quarter(kernel):
    for k, signs in enumerate(((True, True), (False, True), (False, False), (True, False))):
        pl.when(quarter() == k)(functools.partial(kernel, *signs))


def steps(table_ref, i, land, field, eastward, northward):
    p = lax.axis_index("comp")
    high, cols = field.shape
    column = lax.broadcasted_iota(jnp.int32, (1, cols), 1)
    inner = (column != (0 if eastward else cols - 1)).astype(jnp.float32)
    ax = table_ref[p, i]
    ay = table_ref[p, NQ + i]
    stay = 1.0 - ax - ay
    side = inner * ax
    for _ in range(PSTEPS):
        along = pltpu.roll(field, 1 if eastward else cols - 1, 1)
        across = pltpu.roll(field, 1 if northward else high - 1, 0)
        field = (stay * field + side * along + ay * across) * land[...]
    return field


def inner_rows(table_ref, field_ref, mask_ref, mid_ref, land):
    def run(eastward, northward):
        low = 0 if northward else 8
        land[...] = mask_ref[low : low + 24].astype(jnp.float32)

        def component(i, carry):
            f = steps(table_ref, i, land, field_ref[i, low : low + 24] * land[...], eastward, northward)
            mid_ref[i] = f[8 - low : 24 - low]
            return carry

        lax.fori_loop(0, NQ, component, 0)

    by_quarter(run)


def outer_rows(table_ref, field_ref, mask_ref, halo_ref, mid_ref, rim_ref, lo_ref, hi_ref, land, ext):
    def run(eastward, northward):
        halo = 8 - PSTEPS if northward else 24
        rest = 0 if northward else 24 + PSTEPS
        own = ((8, 0), (16, 16), (24, 24)) if northward else ((0, 0), (8, 8), (16, 24))
        zeros = jnp.zeros((8 - PSTEPS, land.shape[1]), jnp.float32)
        land[rest : rest + 8 - PSTEPS] = zeros
        ext[rest : rest + 8 - PSTEPS] = zeros
        land[halo : halo + PSTEPS] = halo_ref[PSTEPS * NQ :]
        for to, row in own:
            land[to : to + 8] = mask_ref[row : row + 8].astype(jnp.float32)

        def component(i, carry):
            for r in range(PSTEPS):
                ext[halo + r : halo + r + 1] = halo_ref[pl.ds(PSTEPS * i + r, 1)]
            for to, row in own:
                ext[to : to + 8] = field_ref[i, row : row + 8] * land[to : to + 8]
            f = steps(table_ref, i, land, ext[...], eastward, northward)
            e0 = f[8:16] if northward else f[0:8]
            e3 = f[24:32] if northward else f[16:24]
            rim_ref[i, 0:8] = e0
            rim_ref[i, 8:16] = e3

            def edge(ref, k):
                ref[k, 0:8] = e0
                ref[k, 8:24] = mid_ref[i]
                ref[k, 24:32] = e3

            pl.when(i < EDGE)(lambda: edge(lo_ref, i))
            pl.when(i >= NQ - EDGE)(lambda: edge(hi_ref, i - (NQ - EDGE)))
            return carry

        lax.fori_loop(0, NQ, component, 0)

    by_quarter(run)


def part_of(mid_ref, rim_ref, t):
    if 8 <= t < 24:
        return mid_ref, pl.ds(t - 8, 8)
    return rim_ref, pl.ds(0 if t < 8 else 8, 8)


def at(low_ref, mid_ref, top_ref, i, rows, edge_rows):
    if i < 0:
        return low_ref[i + EDGE, edge_rows]
    if i >= NQ:
        return top_ref[i - NQ, edge_rows]
    return mid_ref[i, rows]


def sums(table_ref, mid_ref, rim_ref, low_ref, top_ref, ice_ref, thick_ref, out_ref, att_ref):
    fsq = table_ref[lax.axis_index("comp"), 2 * NQ]
    depth = ice_ref[...].astype(jnp.float32) * thick_ref[...]
    att_ref[...] = jnp.exp(-ice_rate * depth * fsq)

    def write(climbed):
        step = 3 if climbed else 1
        for t in range(0, out_ref.shape[1], 8):
            rows = pl.ds(t, 8)
            e_ref, e_rows = part_of(mid_ref, rim_ref, t)
            e = lambda i: at(low_ref, e_ref, top_ref, i, e_rows, rows)
            for i in range(NQ):
                out_ref[i, rows] = e(i - step) + e(i + step)

    by_direction(write)


def half_way(mid_ref, rim_ref, low_ref, top_ref, r_mid_ref, r_rim_ref, share_ref, prev_ref, next_ref):
    rows, cols = low_ref.shape[1:]
    width = cols // GROUP
    for t in range(0, rows, 8):
        there = pl.ds(t, 8)
        e_ref, e_rows = part_of(mid_ref, rim_ref, t)
        r_ref, _ = part_of(r_mid_ref, r_rim_ref, t)
        e = lambda i: at(low_ref, e_ref, top_ref, i, e_rows, there)
        total = jnp.zeros((8, cols), jnp.float32)
        for i in range(NQ):
            around = (e(i - 1) + e(i + 1)) + (e(i - 3) + e(i + 3))
            crossed = 0.25 * mixing_rate * r_ref[i, e_rows] * around
            total = total + (e(i) - mixing_rate * e(i) * e(i) + crossed)
        for g in range(GROUP):
            share_ref[g, there] = total[:, g * width : (g + 1) * width]
        for k in range(EDGE):
            prev_ref[k, there] = r_ref[k, e_rows]
            next_ref[k, there] = r_ref[NQ - EDGE + k, e_rows]


def total_to_all(parts_ref, *refs):
    out_ref = refs[-1]
    total = parts_ref[0]
    for k in range(1, parts_ref.shape[0]):
        total = total + parts_ref[k]
    for k in range(out_ref.shape[0]):
        out_ref[k] = total


def finish(
    table_ref, mid_ref, rim_ref, r_mid_ref, r_rim_ref, low_ref, top_ref, inner_ref, outer_ref, energy_ref, att_ref, out_ref
):
    fsq = table_ref[lax.axis_index("comp"), 2 * NQ]

    def write(climbed, s_ref):
        step = 1 if climbed else 3
        for t in range(0, out_ref.shape[1], 8):
            rows = pl.ds(t, 8)
            e_ref, e_rows = part_of(mid_ref, rim_ref, t)
            r_ref, _ = part_of(r_mid_ref, r_rim_ref, t)
            energy = jnp.concatenate([energy_ref[g, rows] for g in range(GROUP)], axis=1) * (1.0 / (ND * NF))
            factor = att_ref[rows] / (1.0 + whitecap_rate * energy * fsq)
            raw = lambda i: at(low_ref, r_ref, top_ref, i, e_rows, rows)
            for i in range(NQ):
                e = e_ref[i, e_rows]
                around = s_ref[i, rows] + (raw(i - step) + raw(i + step))
                out_ref[i, rows] = (e + mixing_rate * e * (0.25 * around - e)) * factor

    by_place(lambda k: write(k < 2, outer_ref if k in (0, 3) else inner_ref))


def in_vmem(count):
    return [pl.BlockSpec(memory_space=pltpu.VMEM)] * count


def in_smem():
    return [pl.BlockSpec(memory_space=pltpu.SMEM)]


def call(kernel, outs, table, count, scratch=()):
    shapes = [jax.ShapeDtypeStruct(s, jnp.float32) for s in outs]
    specs = in_vmem(len(outs))
    return pl.pallas_call(
        kernel,
        out_shape=shapes,
        in_specs=(in_smem() if table else []) + in_vmem(count),
        out_specs=specs,
        scratch_shapes=list(scratch),
        compiler_params=pltpu.CompilerParams(vmem_limit_bytes=VMEM_BYTES),
        cost_estimate=pl.CostEstimate(flops=1024, bytes_accessed=1024, transcendentals=0),
        name=kernel.__name__,
    )


def body(spectrum, sea_mask, ice_flag, thickness):
    comps, rows, cols = spectrum.shape
    n_comp = lax.axis_size("comp")
    n_space = lax.axis_size("space")
    table = jnp.asarray(tables())

    def place(s):
        return s * Z_LOW // n_space

    def move(value, first, places):
        pairs = []
        for p in range(n_comp):
            for s in range(n_space):
                to = p + (GROUP if climbs(s, n_space) == first else -GROUP)
                if 0 <= to < n_comp and place(s) in places:
                    pairs.append((p * n_space + s, to * n_space + s))
        return lax.ppermute(value, ("comp", "space"), pairs)

    def tell(value):
        pairs = []
        for p in range(n_comp):
            for s in range(n_space):
                if place(s) == 2:
                    pairs.append((p * n_space + s, p * n_space + s + n_space // Z_LOW))
        return lax.ppermute(value, ("comp", "space"), pairs)

    def after(value, *others):
        return lax.optimization_barrier((value, *others))[0]

    def turn(value, step):
        pairs = [(p, p // QUARTERS * QUARTERS + (p + step) % QUARTERS) for p in range(n_comp)]
        return lax.ppermute(value, "comp", pairs)

    message = pl.pallas_call(
        edge_rows,
        grid=(1,),
        out_shape=jax.ShapeDtypeStruct((PSTEPS * (comps + 1), cols), jnp.float32),
        in_specs=[
            pl.BlockSpec((comps, 8, cols), lambda g: (0, 0, 0)),
            pl.BlockSpec((comps, 8, cols), lambda g: (0, rows // 8 - 1, 0)),
            pl.BlockSpec((8, cols), lambda g: (0, 0)),
            pl.BlockSpec((8, cols), lambda g: (rows // 8 - 1, 0)),
        ],
        out_specs=pl.BlockSpec((PSTEPS * (comps + 1), cols), lambda g: (0, 0)),
        name="edge_rows",
    )(spectrum, spectrum, sea_mask, sea_mask)
    pairs = []
    for p in range(n_comp):
        step = 1 if p % QUARTERS < 2 else -1
        pairs += [
            (p * n_space + s, p * n_space + s + step) for s in range(n_space) if 0 <= s + step < n_space
        ]
    halo = lax.ppermute(message, ("comp", "space"), pairs)

    whole = (comps, rows, cols)
    part = (comps, 16, cols)
    edge = (EDGE, rows, cols)

    def land(high):
        return pltpu.VMEM((high, cols), jnp.float32)

    (mid,) = call(inner_rows, [part], True, 2, [land(24)])(table, spectrum, sea_mask)
    r_mid = move(mid, True, (0, 1, 2, 3))
    rim, lo, hi = call(outer_rows, [part, edge, edge], True, 4, [land(32), land(32)])(
        table, spectrum, sea_mask, halo, mid
    )
    r_rim = move(rim, True, (0, 1, 2, 3))
    top = turn(lo, -1)
    low = turn(hi, 1)
    out, att = call(sums, [whole, (rows, cols)], True, 6)(
        table, mid, rim, low, top, ice_flag, thickness
    )
    out, r_mid, r_rim = lax.optimization_barrier((out, r_mid, r_rim))
    inner = move(out, False, (1, 2))

    share, to_prev, to_next = call(half_way, [(GROUP, rows, cols // GROUP), edge, edge], False, 6)(
        mid, rim, low, top, r_mid, r_rim
    )
    near = [list(range(g, g + GROUP)) for g in range(0, n_comp, GROUP)]
    far = [list(range(g, n_comp, GROUP)) for g in range(GROUP)]

    def swap(value, groups):
        return lax.all_to_all(value, "comp", 0, 0, axis_index_groups=groups, tiled=True)

    def spread(value, copies, *others):
        return call(total_to_all, [(copies,) + value.shape[1:]], False, 1 + len(others))(value, *others)[0]

    share = swap(share, near)
    top = turn(after(to_prev, share), -1)
    low = turn(after(to_next, share), 1)
    share = swap(spread(share, n_comp // GROUP), far)
    share, inner = lax.optimization_barrier((share, inner))
    told = tell(share[0])
    out, share, told = lax.optimization_barrier((out, share, told))
    outer = move(out, False, (0, 3))
    energy = swap(spread(share, GROUP, told), near)

    (updated,) = call(finish, [whole], True, 10)(
        table, mid, rim, r_mid, r_rim, low, top, inner, outer, energy, att
    )
    return updated


def solution(mesh):
    in_specs = (P("comp", "space", None), P("space", None), P("space", None), P("space", None))
    out_specs = P("comp", "space", None)
    return jax.shard_map(body, mesh=mesh, in_specs=in_specs, out_specs=out_specs, check_vma=False)
```

```python
import functools
import math

import jax
import jax.numpy as jnp
import numpy as np
from jax import lax
from jax.experimental import pallas as pl
from jax.experimental.pallas import tpu as pltpu
from jax.sharding import PartitionSpec as P

ND = 36
NF = 8
PSTEPS = 4
QUARTERS = 4
NQ = ND // QUARTERS
GROUP = 8
EDGE = 3
Z_LOW = 4

courant_top = 0.65
mixing_rate = 0.5
whitecap_rate = 2.0
ice_rate = 0.3

VMEM_BYTES = 12 * 1024 * 1024


def tables():
    rows = np.zeros((NF * QUARTERS, 2 * NQ + 2), np.float32)
    for p in range(NF * QUARTERS):
        ratio = 1.1 ** (p // QUARTERS)
        for i in range(NQ):
            theta = 2.0 * math.pi * ((p % QUARTERS) * NQ + i + 0.5) / ND
            rows[p, i] = abs(courant_top / ratio * math.cos(theta))
            rows[p, NQ + i] = abs(courant_top / ratio * math.sin(theta))
        rows[p, 2 * NQ] = ratio * ratio
    return rows


def quarter():
    return lax.rem(lax.axis_index("comp"), QUARTERS)


def climbs(space, count):
    return 2 * space < count


def by_direction(kernel):
    here = climbs(lax.axis_index("space"), lax.axis_size("space"))
    pl.when(here)(lambda: kernel(True))
    pl.when(jnp.logical_not(here))(lambda: kernel(False))


def by_place(kernel):
    place = lax.axis_index("space") * Z_LOW // lax.axis_size("space")
    for k in range(Z_LOW):
        pl.when(place == k)(functools.partial(kernel, k))


def edge_rows(first_ref, last_ref, first_mask, last_mask, out_ref):
    def write(field_ref, mask_ref, low):
        land = mask_ref[low : low + PSTEPS].astype(jnp.float32)
        for i in range(NQ):
            out_ref[PSTEPS * i : PSTEPS * (i + 1)] = field_ref[i, low : low + PSTEPS] * land
        out_ref[PSTEPS * NQ :] = land

    @pl.when(quarter() < 2)
    def _():
        write(last_ref, last_mask, 8 - PSTEPS)

    @pl.when(quarter() >= 2)
    def _():
        write(first_ref, first_mask, 0)


def by_quarter(kernel):
    for k, signs in enumerate(((True, True), (False, True), (False, False), (True, False))):
        pl.when(quarter() == k)(functools.partial(kernel, *signs))


def steps(table_ref, i, land, field, eastward, northward):
    p = lax.axis_index("comp")
    high, cols = field.shape
    column = lax.broadcasted_iota(jnp.int32, (1, cols), 1)
    inner = (column != (0 if eastward else cols - 1)).astype(jnp.float32)
    ax = table_ref[p, i]
    ay = table_ref[p, NQ + i]
    stay = 1.0 - ax - ay
    side = inner * ax
    for _ in range(PSTEPS):
        along = pltpu.roll(field, 1 if eastward else cols - 1, 1)
        across = pltpu.roll(field, 1 if northward else high - 1, 0)
        field = (stay * field + side * along + ay * across) * land[...]
    return field


def inner_rows(table_ref, field_ref, mask_ref, mid_ref, land):
    def run(eastward, northward):
        low = 0 if northward else 8
        land[...] = mask_ref[low : low + 24].astype(jnp.float32)

        def component(i, carry):
            f = steps(table_ref, i, land, field_ref[i, low : low + 24] * land[...], eastward, northward)
            mid_ref[i] = f[8 - low : 24 - low]
            return carry

        lax.fori_loop(0, NQ, component, 0, unroll=3)

    by_quarter(run)


def outer_rows(table_ref, field_ref, mask_ref, halo_ref, mid_ref, rim_ref, lo_ref, hi_ref, land, ext):
    def run(eastward, northward):
        halo = 8 - PSTEPS if northward else 24
        rest = 0 if northward else 24 + PSTEPS
        own = ((8, 0), (16, 16), (24, 24)) if northward else ((0, 0), (8, 8), (16, 24))
        zeros = jnp.zeros((8 - PSTEPS, land.shape[1]), jnp.float32)
        land[rest : rest + 8 - PSTEPS] = zeros
        ext[rest : rest + 8 - PSTEPS] = zeros
        land[halo : halo + PSTEPS] = halo_ref[PSTEPS * NQ :]
        for to, row in own:
            land[to : to + 8] = mask_ref[row : row + 8].astype(jnp.float32)

        def component(i, carry):
            for r in range(PSTEPS):
                ext[halo + r : halo + r + 1] = halo_ref[pl.ds(PSTEPS * i + r, 1)]
            for to, row in own:
                ext[to : to + 8] = field_ref[i, row : row + 8] * land[to : to + 8]
            f = steps(table_ref, i, land, ext[...], eastward, northward)
            e0 = f[8:16] if northward else f[0:8]
            e3 = f[24:32] if northward else f[16:24]
            rim_ref[i, 0:8] = e0
            rim_ref[i, 8:16] = e3

            def edge(ref, k):
                ref[k, 0:8] = e0
                ref[k, 8:24] = mid_ref[i]
                ref[k, 24:32] = e3

            pl.when(i < EDGE)(lambda: edge(lo_ref, i))
            pl.when(i >= NQ - EDGE)(lambda: edge(hi_ref, i - (NQ - EDGE)))
            return carry

        lax.fori_loop(0, NQ, component, 0, unroll=3)

    by_quarter(run)


def part_of(mid_ref, rim_ref, t):
    if 8 <= t < 24:
        return mid_ref, pl.ds(t - 8, 8)
    return rim_ref, pl.ds(0 if t < 8 else 8, 8)


def at(low_ref, mid_ref, top_ref, i, rows, edge_rows):
    if i < 0:
        return low_ref[i + EDGE, edge_rows]
    if i >= NQ:
        return top_ref[i - NQ, edge_rows]
    return mid_ref[i, rows]


def sums(table_ref, mid_ref, rim_ref, low_ref, top_ref, ice_ref, thick_ref, out_ref, att_ref):
    fsq = table_ref[lax.axis_index("comp"), 2 * NQ]
    depth = ice_ref[...].astype(jnp.float32) * thick_ref[...]
    att_ref[...] = jnp.exp(-ice_rate * depth * fsq)

    def write(climbed):
        step = 3 if climbed else 1
        for t in range(0, out_ref.shape[1], 8):
            rows = pl.ds(t, 8)
            e_ref, e_rows = part_of(mid_ref, rim_ref, t)
            e = lambda i: at(low_ref, e_ref, top_ref, i, e_rows, rows)
            for i in range(NQ):
                out_ref[i, rows] = e(i - step) + e(i + step)

    by_direction(write)


def half_way(mid_ref, rim_ref, low_ref, top_ref, r_mid_ref, r_rim_ref, share_ref, prev_ref, next_ref):
    rows, cols = low_ref.shape[1:]
    width = cols // GROUP
    for t in range(0, rows, 8):
        there = pl.ds(t, 8)
        e_ref, e_rows = part_of(mid_ref, rim_ref, t)
        r_ref, _ = part_of(r_mid_ref, r_rim_ref, t)
        e = lambda i: at(low_ref, e_ref, top_ref, i, e_rows, there)
        total = jnp.zeros((8, cols), jnp.float32)
        for i in range(NQ):
            around = (e(i - 1) + e(i + 1)) + (e(i - 3) + e(i + 3))
            crossed = 0.25 * mixing_rate * r_ref[i, e_rows] * around
            total = total + (e(i) - mixing_rate * e(i) * e(i) + crossed)
        for g in range(GROUP):
            share_ref[g, there] = total[:, g * width : (g + 1) * width]
        for k in range(EDGE):
            prev_ref[k, there] = r_ref[k, e_rows]
            next_ref[k, there] = r_ref[NQ - EDGE + k, e_rows]


def total_to_all(parts_ref, *refs):
    out_ref = refs[-1]
    total = parts_ref[0]
    for k in range(1, parts_ref.shape[0]):
        total = total + parts_ref[k]
    for k in range(out_ref.shape[0]):
        out_ref[k] = total


def prepare(table_ref, mid_ref, rim_ref, r_mid_ref, r_rim_ref, low_ref, top_ref, energy_ref, att_ref, base_ref, coef_ref):
    fsq = table_ref[lax.axis_index("comp"), 2 * NQ]

    def write(climbed):
        step = 1 if climbed else 3
        for t in range(0, base_ref.shape[1], 8):
            rows = pl.ds(t, 8)
            e_ref, e_rows = part_of(mid_ref, rim_ref, t)
            r_ref, _ = part_of(r_mid_ref, r_rim_ref, t)
            energy = jnp.concatenate([energy_ref[g, rows] for g in range(GROUP)], axis=1) * (1.0 / (ND * NF))
            factor = att_ref[rows] / (1.0 + whitecap_rate * energy * fsq)
            raw = lambda i: at(low_ref, r_ref, top_ref, i, e_rows, rows)
            for i in range(NQ):
                e = e_ref[i, e_rows]
                pair = raw(i - step) + raw(i + step)
                base_ref[i, rows] = (e + mixing_rate * e * (0.25 * pair - e)) * factor
                coef_ref[i, rows] = (0.25 * mixing_rate) * e * factor

    by_direction(write)


def finish(base_ref, coef_ref, inner_ref, outer_ref, out_ref, sums_ref, done_ref, in_sems, out_sems):
    tiles = base_ref.shape[1] // 8

    def fetch(ref, t):
        rows = pl.ds(8 * t, 8)
        return pltpu.make_async_copy(ref.at[:, rows], sums_ref.at[:, rows], in_sems.at[t])

    def store(t):
        rows = pl.ds(8 * t, 8)
        return pltpu.make_async_copy(done_ref.at[:, rows], out_ref.at[:, rows], out_sems.at[t])

    def start(k):
        for t in range(tiles):
            fetch(outer_ref if k in (0, 3) else inner_ref, t).start()

    by_place(start)
    for t in range(tiles):
        rows = pl.ds(8 * t, 8)
        fetch(inner_ref, t).wait()
        for i in range(NQ):
            done_ref[i, rows] = base_ref[i, rows] + coef_ref[i, rows] * sums_ref[i, rows]
        store(t).start()
    for t in range(tiles):
        store(t).wait()


def in_vmem(count):
    return [pl.BlockSpec(memory_space=pltpu.VMEM)] * count


def in_smem():
    return [pl.BlockSpec(memory_space=pltpu.SMEM)]


def call(kernel, outs, table, count, scratch=()):
    shapes = [jax.ShapeDtypeStruct(s, jnp.float32) for s in outs]
    specs = in_vmem(len(outs))
    return pl.pallas_call(
        kernel,
        out_shape=shapes,
        in_specs=(in_smem() if table else []) + in_vmem(count),
        out_specs=specs,
        scratch_shapes=list(scratch),
        compiler_params=pltpu.CompilerParams(vmem_limit_bytes=VMEM_BYTES),
        cost_estimate=pl.CostEstimate(flops=1024, bytes_accessed=1024, transcendentals=0),
        name=kernel.__name__,
    )


def body(spectrum, sea_mask, ice_flag, thickness):
    comps, rows, cols = spectrum.shape
    n_comp = lax.axis_size("comp")
    n_space = lax.axis_size("space")
    table = jnp.asarray(tables())

    def place(s):
        return s * Z_LOW // n_space

    def move(value, first, places):
        pairs = []
        for p in range(n_comp):
            for s in range(n_space):
                to = p + (GROUP if climbs(s, n_space) == first else -GROUP)
                if 0 <= to < n_comp and place(s) in places:
                    pairs.append((p * n_space + s, to * n_space + s))
        return lax.ppermute(value, ("comp", "space"), pairs)

    def tell(value):
        pairs = []
        for p in range(n_comp):
            for s in range(n_space):
                if place(s) == 2:
                    pairs.append((p * n_space + s, p * n_space + s + n_space // Z_LOW))
        return lax.ppermute(value, ("comp", "space"), pairs)

    def after(value, *others):
        return lax.optimization_barrier((value, *others))[0]

    def turn(value, step):
        pairs = [(p, p // QUARTERS * QUARTERS + (p + step) % QUARTERS) for p in range(n_comp)]
        return lax.ppermute(value, "comp", pairs)

    message = pl.pallas_call(
        edge_rows,
        grid=(1,),
        out_shape=jax.ShapeDtypeStruct((PSTEPS * (comps + 1), cols), jnp.float32),
        in_specs=[
            pl.BlockSpec((comps, 8, cols), lambda g: (0, 0, 0)),
            pl.BlockSpec((comps, 8, cols), lambda g: (0, rows // 8 - 1, 0)),
            pl.BlockSpec((8, cols), lambda g: (0, 0)),
            pl.BlockSpec((8, cols), lambda g: (rows // 8 - 1, 0)),
        ],
        out_specs=pl.BlockSpec((PSTEPS * (comps + 1), cols), lambda g: (0, 0)),
        name="edge_rows",
    )(spectrum, spectrum, sea_mask, sea_mask)
    pairs = []
    for p in range(n_comp):
        step = 1 if p % QUARTERS < 2 else -1
        pairs += [
            (p * n_space + s, p * n_space + s + step) for s in range(n_space) if 0 <= s + step < n_space
        ]
    halo = lax.ppermute(message, ("comp", "space"), pairs)

    whole = (comps, rows, cols)
    part = (comps, 16, cols)
    edge = (EDGE, rows, cols)

    def land(high):
        return pltpu.VMEM((high, cols), jnp.float32)

    (mid,) = call(inner_rows, [part], True, 2, [land(24)])(table, spectrum, sea_mask)
    r_mid = move(mid, True, (0, 1, 2, 3))
    rim, lo, hi = call(outer_rows, [part, edge, edge], True, 4, [land(32), land(32)])(
        table, spectrum, sea_mask, halo, mid
    )
    r_rim = move(rim, True, (0, 1, 2, 3))
    top = turn(lo, -1)
    low = turn(hi, 1)
    out, att = call(sums, [whole, (rows, cols)], True, 6)(
        table, mid, rim, low, top, ice_flag, thickness
    )
    out, r_mid, r_rim = lax.optimization_barrier((out, r_mid, r_rim))
    inner = move(out, False, (1, 2))

    share, to_prev, to_next = call(half_way, [(GROUP, rows, cols // GROUP), edge, edge], False, 6)(
        mid, rim, low, top, r_mid, r_rim
    )
    near = [list(range(g, g + GROUP)) for g in range(0, n_comp, GROUP)]
    far = [list(range(g, n_comp, GROUP)) for g in range(GROUP)]

    def swap(value, groups):
        return lax.all_to_all(value, "comp", 0, 0, axis_index_groups=groups, tiled=True)

    def spread(value, copies, *others):
        return call(total_to_all, [(copies,) + value.shape[1:]], False, 1 + len(others))(value, *others)[0]

    share = swap(share, near)
    top = turn(after(to_prev, share), -1)
    low = turn(after(to_next, share), 1)
    share = swap(spread(share, n_comp // GROUP), far)
    share, inner = lax.optimization_barrier((share, inner))
    told = tell(share[0])
    out, share, told = lax.optimization_barrier((out, share, told))
    outer = move(out, False, (0, 3))
    energy = swap(spread(share, GROUP, told), near)

    base, coef = call(prepare, [whole, whole], True, 8)(
        table, mid, rim, r_mid, r_rim, low, top, energy, att
    )
    anywhere = pl.BlockSpec(memory_space=pl.ANY)
    return pl.pallas_call(
        finish,
        out_shape=jax.ShapeDtypeStruct(whole, jnp.float32),
        in_specs=in_vmem(2) + [anywhere, anywhere],
        out_specs=anywhere,
        scratch_shapes=[
            pltpu.VMEM(whole, jnp.float32),
            pltpu.VMEM(whole, jnp.float32),
            pltpu.SemaphoreType.DMA((rows // 8,)),
            pltpu.SemaphoreType.DMA((rows // 8,)),
        ],
        compiler_params=pltpu.CompilerParams(vmem_limit_bytes=VMEM_BYTES),
        name="finish",
    )(base, coef, inner, outer)


def solution(mesh):
    in_specs = (P("comp", "space", None), P("space", None), P("space", None), P("space", None))
    out_specs = P("comp", "space", None)
    return jax.shard_map(body, mesh=mesh, in_specs=in_specs, out_specs=out_specs, check_vma=False)
```

```python
import functools
import math

import jax
import jax.numpy as jnp
import numpy as np
from jax import lax
from jax.experimental import pallas as pl
from jax.experimental.pallas import tpu as pltpu
from jax.sharding import PartitionSpec as P

ND = 36
NF = 8
PSTEPS = 4
QUARTERS = 4
NQ = ND // QUARTERS
GROUP = 8
EDGE = 3
Z_LOW = 4

courant_top = 0.65
mixing_rate = 0.5
whitecap_rate = 2.0
ice_rate = 0.3

VMEM_BYTES = 12 * 1024 * 1024


def tables():
    rows = np.zeros((NF * QUARTERS, 2 * NQ + 2), np.float32)
    for p in range(NF * QUARTERS):
        ratio = 1.1 ** (p // QUARTERS)
        for i in range(NQ):
            theta = 2.0 * math.pi * ((p % QUARTERS) * NQ + i + 0.5) / ND
            rows[p, i] = abs(courant_top / ratio * math.cos(theta))
            rows[p, NQ + i] = abs(courant_top / ratio * math.sin(theta))
        rows[p, 2 * NQ] = ratio * ratio
    return rows


def quarter():
    return lax.rem(lax.axis_index("comp"), QUARTERS)


def climbs(space, count):
    return 2 * space < count


def by_direction(kernel):
    here = climbs(lax.axis_index("space"), lax.axis_size("space"))
    pl.when(here)(lambda: kernel(True))
    pl.when(jnp.logical_not(here))(lambda: kernel(False))


def by_place(kernel):
    place = lax.axis_index("space") * Z_LOW // lax.axis_size("space")
    for k in range(Z_LOW):
        pl.when(place == k)(functools.partial(kernel, k))


def edge_rows(first_ref, last_ref, first_mask, last_mask, out_ref):
    def write(field_ref, mask_ref, low):
        land = mask_ref[low : low + PSTEPS].astype(jnp.float32)
        for i in range(NQ):
            out_ref[PSTEPS * i : PSTEPS * (i + 1)] = field_ref[i, low : low + PSTEPS] * land
        out_ref[PSTEPS * NQ :] = land

    @pl.when(quarter() < 2)
    def _():
        write(last_ref, last_mask, 8 - PSTEPS)

    @pl.when(quarter() >= 2)
    def _():
        write(first_ref, first_mask, 0)


def by_quarter(kernel):
    for k, signs in enumerate(((True, True), (False, True), (False, False), (True, False))):
        pl.when(quarter() == k)(functools.partial(kernel, *signs))


def steps(table_ref, i, land, field, eastward, northward):
    p = lax.axis_index("comp")
    high, cols = field.shape
    column = lax.broadcasted_iota(jnp.int32, (1, cols), 1)
    inner = (column != (0 if eastward else cols - 1)).astype(jnp.float32)
    ax = table_ref[p, i]
    ay = table_ref[p, NQ + i]
    stay = 1.0 - ax - ay
    side = inner * ax
    for _ in range(PSTEPS):
        along = pltpu.roll(field, 1 if eastward else cols - 1, 1)
        across = pltpu.roll(field, 1 if northward else high - 1, 0)
        field = (stay * field + side * along + ay * across) * land[...]
    return field


def inner_rows(table_ref, field_ref, mask_ref, mid_ref, land):
    def run(eastward, northward):
        low = 0 if northward else 8
        land[...] = mask_ref[low : low + 24].astype(jnp.float32)

        def component(i, carry):
            f = steps(table_ref, i, land, field_ref[i, low : low + 24] * land[...], eastward, northward)
            mid_ref[i] = f[8 - low : 24 - low]
            return carry

        lax.fori_loop(0, NQ, component, 0, unroll=3)

    by_quarter(run)


def outer_rows(table_ref, field_ref, mask_ref, halo_ref, mid_ref, rim_ref, lo_ref, hi_ref, land, ext):
    def run(eastward, northward):
        halo = 8 - PSTEPS if northward else 24
        rest = 0 if northward else 24 + PSTEPS
        own = ((8, 0), (16, 16), (24, 24)) if northward else ((0, 0), (8, 8), (16, 24))
        zeros = jnp.zeros((8 - PSTEPS, land.shape[1]), jnp.float32)
        land[rest : rest + 8 - PSTEPS] = zeros
        ext[rest : rest + 8 - PSTEPS] = zeros
        land[halo : halo + PSTEPS] = halo_ref[PSTEPS * NQ :]
        for to, row in own:
            land[to : to + 8] = mask_ref[row : row + 8].astype(jnp.float32)

        def component(i, carry):
            for r in range(PSTEPS):
                ext[halo + r : halo + r + 1] = halo_ref[pl.ds(PSTEPS * i + r, 1)]
            for to, row in own:
                ext[to : to + 8] = field_ref[i, row : row + 8] * land[to : to + 8]
            f = steps(table_ref, i, land, ext[...], eastward, northward)
            e0 = f[8:16] if northward else f[0:8]
            e3 = f[24:32] if northward else f[16:24]
            rim_ref[i, 0:8] = e0
            rim_ref[i, 8:16] = e3

            def edge(ref, k):
                ref[k, 0:8] = e0
                ref[k, 8:24] = mid_ref[i]
                ref[k, 24:32] = e3

            pl.when(i < EDGE)(lambda: edge(lo_ref, i))
            pl.when(i >= NQ - EDGE)(lambda: edge(hi_ref, i - (NQ - EDGE)))
            return carry

        lax.fori_loop(0, NQ, component, 0, unroll=3)

    by_quarter(run)


def part_of(mid_ref, rim_ref, t):
    if 8 <= t < 24:
        return mid_ref, pl.ds(t - 8, 8)
    return rim_ref, pl.ds(0 if t < 8 else 8, 8)


def at(low_ref, mid_ref, top_ref, i, rows, edge_rows):
    if i < 0:
        return low_ref[i + EDGE, edge_rows]
    if i >= NQ:
        return top_ref[i - NQ, edge_rows]
    return mid_ref[i, rows]


def sums(table_ref, mid_ref, rim_ref, low_ref, top_ref, ice_ref, thick_ref, out_ref, att_ref):
    fsq = table_ref[lax.axis_index("comp"), 2 * NQ]
    depth = ice_ref[...].astype(jnp.float32) * thick_ref[...]
    att_ref[...] = jnp.exp(-ice_rate * depth * fsq)

    def write(climbed):
        step = 3 if climbed else 1
        for t in range(0, out_ref.shape[1], 8):
            rows = pl.ds(t, 8)
            e_ref, e_rows = part_of(mid_ref, rim_ref, t)
            e = lambda i: at(low_ref, e_ref, top_ref, i, e_rows, rows)
            for i in range(NQ):
                out_ref[i, rows] = e(i - step) + e(i + step)

    by_direction(write)


def half_way(mid_ref, rim_ref, low_ref, top_ref, r_mid_ref, r_rim_ref, share_ref, prev_ref, next_ref):
    rows, cols = low_ref.shape[1:]
    width = cols // GROUP
    for t in range(0, rows, 8):
        there = pl.ds(t, 8)
        e_ref, e_rows = part_of(mid_ref, rim_ref, t)
        r_ref, _ = part_of(r_mid_ref, r_rim_ref, t)
        e = lambda i: at(low_ref, e_ref, top_ref, i, e_rows, there)
        total = jnp.zeros((8, cols), jnp.float32)
        for i in range(NQ):
            around = (e(i - 1) + e(i + 1)) + (e(i - 3) + e(i + 3))
            crossed = 0.25 * mixing_rate * r_ref[i, e_rows] * around
            total = total + (e(i) - mixing_rate * e(i) * e(i) + crossed)
        for g in range(GROUP):
            share_ref[g, there] = total[:, g * width : (g + 1) * width]
        for k in range(EDGE):
            prev_ref[k, there] = r_ref[k, e_rows]
            next_ref[k, there] = r_ref[NQ - EDGE + k, e_rows]


def total_to_all(parts_ref, *refs):
    out_ref = refs[-1]
    total = parts_ref[0]
    for k in range(1, parts_ref.shape[0]):
        total = total + parts_ref[k]
    for k in range(out_ref.shape[0]):
        out_ref[k] = total


def prepare(table_ref, mid_ref, rim_ref, r_mid_ref, r_rim_ref, low_ref, top_ref, energy_ref, att_ref, base_ref, coef_ref):
    fsq = table_ref[lax.axis_index("comp"), 2 * NQ]

    def write(climbed):
        step = 1 if climbed else 3
        for t in range(0, base_ref.shape[1], 8):
            rows = pl.ds(t, 8)
            e_ref, e_rows = part_of(mid_ref, rim_ref, t)
            r_ref, _ = part_of(r_mid_ref, r_rim_ref, t)
            energy = jnp.concatenate([energy_ref[g, rows] for g in range(GROUP)], axis=1) * (1.0 / (ND * NF))
            factor = att_ref[rows] / (1.0 + whitecap_rate * energy * fsq)
            raw = lambda i: at(low_ref, r_ref, top_ref, i, e_rows, rows)
            for i in range(NQ):
                e = e_ref[i, e_rows]
                pair = raw(i - step) + raw(i + step)
                base_ref[i, rows] = (e + mixing_rate * e * (0.25 * pair - e)) * factor
                coef_ref[i, rows] = (0.25 * mixing_rate) * e * factor

    by_direction(write)


def finish(base_ref, coef_ref, first_ref, inner_ref, last_ref, out_ref, sums_ref, done_ref, in_sems, out_sems):
    tiles = base_ref.shape[1] // 8

    def fetch(ref, t):
        rows = pl.ds(8 * t, 8)
        return pltpu.make_async_copy(ref.at[:, rows], sums_ref.at[:, rows], in_sems.at[t])

    def store(t):
        rows = pl.ds(8 * t, 8)
        return pltpu.make_async_copy(done_ref.at[:, rows], out_ref.at[:, rows], out_sems.at[t])

    def start(k):
        for t in range(tiles):
            fetch((first_ref, inner_ref, inner_ref, last_ref)[k], t).start()

    by_place(start)
    for t in range(tiles):
        rows = pl.ds(8 * t, 8)
        fetch(inner_ref, t).wait()
        for i in range(NQ):
            done_ref[i, rows] = base_ref[i, rows] + coef_ref[i, rows] * sums_ref[i, rows]
        store(t).start()
    for t in range(tiles):
        store(t).wait()


def in_vmem(count):
    return [pl.BlockSpec(memory_space=pltpu.VMEM)] * count


def in_smem():
    return [pl.BlockSpec(memory_space=pltpu.SMEM)]


def call(kernel, outs, table, count, scratch=()):
    shapes = [jax.ShapeDtypeStruct(s, jnp.float32) for s in outs]
    specs = in_vmem(len(outs))
    return pl.pallas_call(
        kernel,
        out_shape=shapes,
        in_specs=(in_smem() if table else []) + in_vmem(count),
        out_specs=specs,
        scratch_shapes=list(scratch),
        compiler_params=pltpu.CompilerParams(vmem_limit_bytes=VMEM_BYTES),
        cost_estimate=pl.CostEstimate(flops=1024, bytes_accessed=1024, transcendentals=0),
        name=kernel.__name__,
    )


def body(spectrum, sea_mask, ice_flag, thickness):
    comps, rows, cols = spectrum.shape
    n_comp = lax.axis_size("comp")
    n_space = lax.axis_size("space")
    table = jnp.asarray(tables())

    def place(s):
        return s * Z_LOW // n_space

    def move(value, first, places):
        pairs = []
        for p in range(n_comp):
            for s in range(n_space):
                to = p + (GROUP if climbs(s, n_space) == first else -GROUP)
                if 0 <= to < n_comp and place(s) in places:
                    pairs.append((p * n_space + s, to * n_space + s))
        return lax.ppermute(value, ("comp", "space"), pairs)

    def tell(value):
        pairs = []
        for p in range(n_comp):
            for s in range(n_space):
                if place(s) == 2:
                    pairs.append((p * n_space + s, p * n_space + s + n_space // Z_LOW))
        return lax.ppermute(value, ("comp", "space"), pairs)

    def after(value, *others):
        return lax.optimization_barrier((value, *others))[0]

    def turn(value, step):
        pairs = [(p, p // QUARTERS * QUARTERS + (p + step) % QUARTERS) for p in range(n_comp)]
        return lax.ppermute(value, "comp", pairs)

    message = pl.pallas_call(
        edge_rows,
        grid=(1,),
        out_shape=jax.ShapeDtypeStruct((PSTEPS * (comps + 1), cols), jnp.float32),
        in_specs=[
            pl.BlockSpec((comps, 8, cols), lambda g: (0, 0, 0)),
            pl.BlockSpec((comps, 8, cols), lambda g: (0, rows // 8 - 1, 0)),
            pl.BlockSpec((8, cols), lambda g: (0, 0)),
            pl.BlockSpec((8, cols), lambda g: (rows // 8 - 1, 0)),
        ],
        out_specs=pl.BlockSpec((PSTEPS * (comps + 1), cols), lambda g: (0, 0)),
        name="edge_rows",
    )(spectrum, spectrum, sea_mask, sea_mask)
    pairs = []
    for p in range(n_comp):
        step = 1 if p % QUARTERS < 2 else -1
        pairs += [
            (p * n_space + s, p * n_space + s + step) for s in range(n_space) if 0 <= s + step < n_space
        ]
    halo = lax.ppermute(message, ("comp", "space"), pairs)

    whole = (comps, rows, cols)
    part = (comps, 16, cols)
    edge = (EDGE, rows, cols)

    def land(high):
        return pltpu.VMEM((high, cols), jnp.float32)

    (mid,) = call(inner_rows, [part], True, 2, [land(24)])(table, spectrum, sea_mask)
    r_mid = move(mid, True, (0, 1, 2, 3))
    rim, lo, hi = call(outer_rows, [part, edge, edge], True, 4, [land(32), land(32)])(
        table, spectrum, sea_mask, halo, mid
    )
    r_rim = move(rim, True, (0, 1, 2, 3))
    top = turn(lo, -1)
    low = turn(hi, 1)
    out, att = call(sums, [whole, (rows, cols)], True, 6)(
        table, mid, rim, low, top, ice_flag, thickness
    )
    out, r_mid, r_rim = lax.optimization_barrier((out, r_mid, r_rim))
    inner = move(out, False, (1, 2))
    first = move(out, False, (0,))

    share, to_prev, to_next = call(half_way, [(GROUP, rows, cols // GROUP), edge, edge], False, 6)(
        mid, rim, low, top, r_mid, r_rim
    )
    near = [list(range(g, g + GROUP)) for g in range(0, n_comp, GROUP)]
    far = [list(range(g, n_comp, GROUP)) for g in range(GROUP)]

    def swap(value, groups):
        return lax.all_to_all(value, "comp", 0, 0, axis_index_groups=groups, tiled=True)

    def spread(value, copies, *others):
        return call(total_to_all, [(copies,) + value.shape[1:]], False, 1 + len(others))(value, *others)[0]

    share = swap(share, near)
    top = turn(after(to_prev, share), -1)
    low = turn(after(to_next, share), 1)
    share = swap(spread(share, n_comp // GROUP), far)
    share, word = lax.optimization_barrier((share, inner[0, :8, :128]))
    told = tell(word)
    out, share, told = lax.optimization_barrier((out, share, told))
    last = move(out, False, (3,))
    energy = swap(spread(share, GROUP, told), near)

    base, coef = call(prepare, [whole, whole], True, 8)(
        table, mid, rim, r_mid, r_rim, low, top, energy, att
    )
    anywhere = pl.BlockSpec(memory_space=pl.ANY)
    return pl.pallas_call(
        finish,
        out_shape=jax.ShapeDtypeStruct(whole, jnp.float32),
        in_specs=in_vmem(2) + [anywhere] * 3,
        out_specs=anywhere,
        scratch_shapes=[
            pltpu.VMEM(whole, jnp.float32),
            pltpu.VMEM(whole, jnp.float32),
            pltpu.SemaphoreType.DMA((rows // 8,)),
            pltpu.SemaphoreType.DMA((rows // 8,)),
        ],
        compiler_params=pltpu.CompilerParams(vmem_limit_bytes=VMEM_BYTES),
        name="finish",
    )(base, coef, first, inner, last)


def solution(mesh):
    in_specs = (P("comp", "space", None), P("space", None), P("space", None), P("space", None))
    out_specs = P("comp", "space", None)
    return jax.shard_map(body, mesh=mesh, in_specs=in_specs, out_specs=out_specs, check_vma=False)
```

```python
import functools
import math

import jax
import jax.numpy as jnp
import numpy as np
from jax import lax
from jax.experimental import pallas as pl
from jax.experimental.pallas import tpu as pltpu
from jax.sharding import PartitionSpec as P

ND = 36
NF = 8
PSTEPS = 4
QUARTERS = 4
NQ = ND // QUARTERS
GROUP = 8
EDGE = 3
Z_LOW = 4

courant_top = 0.65
mixing_rate = 0.5
whitecap_rate = 2.0
ice_rate = 0.3

VMEM_BYTES = 12 * 1024 * 1024


def tables():
    rows = np.zeros((NF * QUARTERS, 2 * NQ + 2), np.float32)
    for p in range(NF * QUARTERS):
        ratio = 1.1 ** (p // QUARTERS)
        for i in range(NQ):
            theta = 2.0 * math.pi * ((p % QUARTERS) * NQ + i + 0.5) / ND
            rows[p, i] = abs(courant_top / ratio * math.cos(theta))
            rows[p, NQ + i] = abs(courant_top / ratio * math.sin(theta))
        rows[p, 2 * NQ] = ratio * ratio
    return rows


def quarter():
    return lax.rem(lax.axis_index("comp"), QUARTERS)


def climbs(space, count):
    return 2 * space < count


def by_direction(kernel):
    here = climbs(lax.axis_index("space"), lax.axis_size("space"))
    pl.when(here)(lambda: kernel(True))
    pl.when(jnp.logical_not(here))(lambda: kernel(False))


def by_place(kernel):
    place = lax.axis_index("space") * Z_LOW // lax.axis_size("space")
    for k in range(Z_LOW):
        pl.when(place == k)(functools.partial(kernel, k))


def edge_rows(field_ref, mask_ref, out_ref, field, mask, sems):
    def write(start, low):
        copies = [
            pltpu.make_async_copy(field_ref.at[:, pl.ds(start, 8)], field, sems.at[0]),
            pltpu.make_async_copy(mask_ref.at[pl.ds(start, 8)], mask, sems.at[1]),
        ]
        for copy in copies:
            copy.start()
        for copy in copies:
            copy.wait()
        land = mask[low : low + PSTEPS].astype(jnp.float32)
        for i in range(NQ):
            out_ref[PSTEPS * i : PSTEPS * (i + 1)] = field[i, low : low + PSTEPS] * land
        out_ref[PSTEPS * NQ :] = land

    pl.when(quarter() < 2)(lambda: write(field_ref.shape[1] - 8, 8 - PSTEPS))
    pl.when(quarter() >= 2)(lambda: write(0, 0))


def by_quarter(kernel):
    for k, signs in enumerate(((True, True), (False, True), (False, False), (True, False))):
        pl.when(quarter() == k)(functools.partial(kernel, *signs))


def steps(table_ref, i, land, field, eastward, northward):
    p = lax.axis_index("comp")
    high, cols = field.shape
    column = lax.broadcasted_iota(jnp.int32, (1, cols), 1)
    inner = (column != (0 if eastward else cols - 1)).astype(jnp.float32)
    ax = table_ref[p, i]
    ay = table_ref[p, NQ + i]
    stay = 1.0 - ax - ay
    side = inner * ax
    for _ in range(PSTEPS):
        along = pltpu.roll(field, 1 if eastward else cols - 1, 1)
        across = pltpu.roll(field, 1 if northward else high - 1, 0)
        field = (stay * field + side * along + ay * across) * land[...]
    return field


def inner_rows(table_ref, field_ref, mask_ref, mid_ref, land):
    def run(eastward, northward):
        low = 0 if northward else 8
        land[...] = mask_ref[low : low + 24].astype(jnp.float32)

        def component(i, carry):
            f = steps(table_ref, i, land, field_ref[i, low : low + 24] * land[...], eastward, northward)
            mid_ref[i] = f[8 - low : 24 - low]
            return carry

        lax.fori_loop(0, NQ, component, 0, unroll=3)

    by_quarter(run)


def outer_rows(table_ref, field_ref, mask_ref, halo_ref, mid_ref, rim_ref, lo_ref, hi_ref, land, ext):
    def run(eastward, northward):
        halo = 8 - PSTEPS if northward else 24
        rest = 0 if northward else 24 + PSTEPS
        own = ((8, 0), (16, 16), (24, 24)) if northward else ((0, 0), (8, 8), (16, 24))
        zeros = jnp.zeros((8 - PSTEPS, land.shape[1]), jnp.float32)
        land[rest : rest + 8 - PSTEPS] = zeros
        ext[rest : rest + 8 - PSTEPS] = zeros
        land[halo : halo + PSTEPS] = halo_ref[PSTEPS * NQ :]
        for to, row in own:
            land[to : to + 8] = mask_ref[row : row + 8].astype(jnp.float32)

        def component(i, carry):
            for r in range(PSTEPS):
                ext[halo + r : halo + r + 1] = halo_ref[pl.ds(PSTEPS * i + r, 1)]
            for to, row in own:
                ext[to : to + 8] = field_ref[i, row : row + 8] * land[to : to + 8]
            f = steps(table_ref, i, land, ext[...], eastward, northward)
            e0 = f[8:16] if northward else f[0:8]
            e3 = f[24:32] if northward else f[16:24]
            rim_ref[i, 0:8] = e0
            rim_ref[i, 8:16] = e3

            def edge(ref, k):
                ref[k, 0:8] = e0
                ref[k, 8:24] = mid_ref[i]
                ref[k, 24:32] = e3

            pl.when(i < EDGE)(lambda: edge(lo_ref, i))
            pl.when(i >= NQ - EDGE)(lambda: edge(hi_ref, i - (NQ - EDGE)))
            return carry

        lax.fori_loop(0, NQ, component, 0, unroll=3)

    by_quarter(run)


def part_of(mid_ref, rim_ref, t):
    if 8 <= t < 24:
        return mid_ref, pl.ds(t - 8, 8)
    return rim_ref, pl.ds(0 if t < 8 else 8, 8)


def at(low_ref, mid_ref, top_ref, i, rows, edge_rows):
    if i < 0:
        return low_ref[i + EDGE, edge_rows]
    if i >= NQ:
        return top_ref[i - NQ, edge_rows]
    return mid_ref[i, rows]


def sums(table_ref, mid_ref, rim_ref, low_ref, top_ref, ice_ref, thick_ref, out_ref, att_ref):
    fsq = table_ref[lax.axis_index("comp"), 2 * NQ]
    depth = ice_ref[...].astype(jnp.float32) * thick_ref[...]
    att_ref[...] = jnp.exp(-ice_rate * depth * fsq)

    def write(climbed):
        step = 3 if climbed else 1
        for t in range(0, out_ref.shape[1], 8):
            rows = pl.ds(t, 8)
            e_ref, e_rows = part_of(mid_ref, rim_ref, t)
            e = lambda i: at(low_ref, e_ref, top_ref, i, e_rows, rows)
            for i in range(NQ):
                out_ref[i, rows] = e(i - step) + e(i + step)

    by_direction(write)


def half_way(mid_ref, rim_ref, low_ref, top_ref, r_mid_ref, r_rim_ref, share_ref, prev_ref, next_ref):
    rows, cols = low_ref.shape[1:]
    width = cols // GROUP
    for t in range(0, rows, 8):
        there = pl.ds(t, 8)
        e_ref, e_rows = part_of(mid_ref, rim_ref, t)
        r_ref, _ = part_of(r_mid_ref, r_rim_ref, t)
        e = lambda i: at(low_ref, e_ref, top_ref, i, e_rows, there)
        total = jnp.zeros((8, cols), jnp.float32)
        for i in range(NQ):
            around = (e(i - 1) + e(i + 1)) + (e(i - 3) + e(i + 3))
            crossed = 0.25 * mixing_rate * r_ref[i, e_rows] * around
            total = total + (e(i) - mixing_rate * e(i) * e(i) + crossed)
        for g in range(GROUP):
            share_ref[g, there] = total[:, g * width : (g + 1) * width]
        for k in range(EDGE):
            prev_ref[k, there] = r_ref[k, e_rows]
            next_ref[k, there] = r_ref[NQ - EDGE + k, e_rows]


def total_to_all(parts_ref, *refs):
    out_ref = refs[-1]
    total = parts_ref[0]
    for k in range(1, parts_ref.shape[0]):
        total = total + parts_ref[k]
    for k in range(out_ref.shape[0]):
        out_ref[k] = total


def prepare(table_ref, mid_ref, rim_ref, r_mid_ref, r_rim_ref, low_ref, top_ref, energy_ref, att_ref, base_ref, coef_ref):
    fsq = table_ref[lax.axis_index("comp"), 2 * NQ]

    def write(climbed):
        step = 1 if climbed else 3
        for t in range(0, base_ref.shape[1], 8):
            rows = pl.ds(t, 8)
            e_ref, e_rows = part_of(mid_ref, rim_ref, t)
            r_ref, _ = part_of(r_mid_ref, r_rim_ref, t)
            energy = jnp.concatenate([energy_ref[g, rows] for g in range(GROUP)], axis=1) * (1.0 / (ND * NF))
            factor = att_ref[rows] / (1.0 + whitecap_rate * energy * fsq)
            raw = lambda i: at(low_ref, r_ref, top_ref, i, e_rows, rows)
            for i in range(NQ):
                e = e_ref[i, e_rows]
                pair = raw(i - step) + raw(i + step)
                base_ref[i, rows] = (e + mixing_rate * e * (0.25 * pair - e)) * factor
                coef_ref[i, rows] = (0.25 * mixing_rate) * e * factor

    by_direction(write)


def finish(base_ref, coef_ref, first_ref, inner_ref, last_ref, out_ref, sums_ref, done_ref, in_sems, out_sems):
    tiles = base_ref.shape[1] // 8

    def fetch(ref, t):
        rows = pl.ds(8 * t, 8)
        return pltpu.make_async_copy(ref.at[:, rows], sums_ref.at[:, rows], in_sems.at[t])

    def store(t):
        rows = pl.ds(8 * t, 8)
        return pltpu.make_async_copy(done_ref.at[:, rows], out_ref.at[:, rows], out_sems.at[t])

    def start(k):
        for t in range(tiles):
            fetch((first_ref, inner_ref, inner_ref, last_ref)[k], t).start()

    by_place(start)
    for t in range(tiles):
        rows = pl.ds(8 * t, 8)
        fetch(inner_ref, t).wait()
        for i in range(NQ):
            done_ref[i, rows] = base_ref[i, rows] + coef_ref[i, rows] * sums_ref[i, rows]
        store(t).start()
    for t in range(tiles):
        store(t).wait()


def in_vmem(count):
    return [pl.BlockSpec(memory_space=pltpu.VMEM)] * count


def in_smem():
    return [pl.BlockSpec(memory_space=pltpu.SMEM)]


def call(kernel, outs, table, count, scratch=()):
    shapes = [jax.ShapeDtypeStruct(s, jnp.float32) for s in outs]
    specs = in_vmem(len(outs))
    return pl.pallas_call(
        kernel,
        out_shape=shapes,
        in_specs=(in_smem() if table else []) + in_vmem(count),
        out_specs=specs,
        scratch_shapes=list(scratch),
        compiler_params=pltpu.CompilerParams(vmem_limit_bytes=VMEM_BYTES),
        cost_estimate=pl.CostEstimate(flops=1024, bytes_accessed=1024, transcendentals=0),
        name=kernel.__name__,
    )


def body(spectrum, sea_mask, ice_flag, thickness):
    comps, rows, cols = spectrum.shape
    n_comp = lax.axis_size("comp")
    n_space = lax.axis_size("space")
    table = jnp.asarray(tables())

    def place(s):
        return s * Z_LOW // n_space

    def move(value, first, places):
        pairs = []
        for p in range(n_comp):
            for s in range(n_space):
                to = p + (GROUP if climbs(s, n_space) == first else -GROUP)
                if 0 <= to < n_comp and place(s) in places:
                    pairs.append((p * n_space + s, to * n_space + s))
        return lax.ppermute(value, ("comp", "space"), pairs)

    def tell(value):
        pairs = []
        for p in range(n_comp):
            for s in range(n_space):
                if place(s) == 2:
                    pairs.append((p * n_space + s, p * n_space + s + n_space // Z_LOW))
        return lax.ppermute(value, ("comp", "space"), pairs)

    def after(value, *others):
        return lax.optimization_barrier((value, *others))[0]

    def turn(value, step):
        pairs = [(p, p // QUARTERS * QUARTERS + (p + step) % QUARTERS) for p in range(n_comp)]
        return lax.ppermute(value, "comp", pairs)

    message = pl.pallas_call(
        edge_rows,
        out_shape=jax.ShapeDtypeStruct((PSTEPS * (comps + 1), cols), jnp.float32),
        in_specs=[pl.BlockSpec(memory_space=pl.ANY)] * 2,
        out_specs=pl.BlockSpec(memory_space=pltpu.VMEM),
        scratch_shapes=[
            pltpu.VMEM((comps, 8, cols), jnp.float32),
            pltpu.VMEM((8, cols), jnp.int32),
            pltpu.SemaphoreType.DMA((2,)),
        ],
        compiler_params=pltpu.CompilerParams(vmem_limit_bytes=VMEM_BYTES),
        name="edge_rows",
    )(spectrum, sea_mask)
    pairs = []
    for p in range(n_comp):
        step = 1 if p % QUARTERS < 2 else -1
        pairs += [
            (p * n_space + s, p * n_space + s + step) for s in range(n_space) if 0 <= s + step < n_space
        ]
    halo = lax.ppermute(message, ("comp", "space"), pairs)

    whole = (comps, rows, cols)
    part = (comps, 16, cols)
    edge = (EDGE, rows, cols)

    def land(high):
        return pltpu.VMEM((high, cols), jnp.float32)

    (mid,) = call(inner_rows, [part], True, 2, [land(24)])(table, spectrum, sea_mask)
    r_mid = move(mid, True, (0, 1, 2, 3))
    rim, lo, hi = call(outer_rows, [part, edge, edge], True, 4, [land(32), land(32)])(
        table, spectrum, sea_mask, halo, mid
    )
    r_rim = move(rim, True, (0, 1, 2, 3))
    top = turn(lo, -1)
    low = turn(hi, 1)
    out, att = call(sums, [whole, (rows, cols)], True, 6)(
        table, mid, rim, low, top, ice_flag, thickness
    )
    out, r_mid, r_rim = lax.optimization_barrier((out, r_mid, r_rim))
    inner = move(out, False, (1, 2))
    first = move(out, False, (0,))

    share, to_prev, to_next = call(half_way, [(GROUP, rows, cols // GROUP), edge, edge], False, 6)(
        mid, rim, low, top, r_mid, r_rim
    )
    near = [list(range(g, g + GROUP)) for g in range(0, n_comp, GROUP)]
    far = [list(range(g, n_comp, GROUP)) for g in range(GROUP)]

    def swap(value, groups):
        return lax.all_to_all(value, "comp", 0, 0, axis_index_groups=groups, tiled=True)

    def spread(value, copies, *others):
        return call(total_to_all, [(copies,) + value.shape[1:]], False, 1 + len(others))(value, *others)[0]

    share = swap(share, near)
    top = turn(after(to_prev, share), -1)
    low = turn(after(to_next, share), 1)
    share = swap(spread(share, n_comp // GROUP), far)
    share, word = lax.optimization_barrier((share, inner[0, :8, :128]))
    told = tell(word)
    out, share, told = lax.optimization_barrier((out, share, told))
    last = move(out, False, (3,))
    energy = swap(spread(share, GROUP, told), near)

    base, coef = call(prepare, [whole, whole], True, 8)(
        table, mid, rim, r_mid, r_rim, low, top, energy, att
    )
    anywhere = pl.BlockSpec(memory_space=pl.ANY)
    return pl.pallas_call(
        finish,
        out_shape=jax.ShapeDtypeStruct(whole, jnp.float32),
        in_specs=in_vmem(2) + [anywhere] * 3,
        out_specs=anywhere,
        scratch_shapes=[
            pltpu.VMEM(whole, jnp.float32),
            pltpu.VMEM(whole, jnp.float32),
            pltpu.SemaphoreType.DMA((rows // 8,)),
            pltpu.SemaphoreType.DMA((rows // 8,)),
        ],
        compiler_params=pltpu.CompilerParams(vmem_limit_bytes=VMEM_BYTES),
        name="finish",
    )(base, coef, first, inner, last)


def solution(mesh):
    in_specs = (P("comp", "space", None), P("space", None), P("space", None), P("space", None))
    out_specs = P("comp", "space", None)
    return jax.shard_map(body, mesh=mesh, in_specs=in_specs, out_specs=out_specs, check_vma=False)
```
